32 devices in a mesh: group: 2 (over y), fsdp: 16 (over z, x, core).
Axes of the slice: x: 2, y: 2, z: 4, core: 2. Of those that a mesh axis runs over, the one named last changes fastest.
Arguments:
- hidden: bfloat16 [2, 32, 256, 5120], P('group', 'fsdp'), may hold values from -600 to 600
- norm_gain: float32 [5120], replicated, may hold values from 0.1 to 1.9
- queries: bfloat16 [2, 32, 256, 2560], P('group', 'fsdp'), may hold values from -800 to 800
- out_grad: bfloat16 [2, 32, 256, 2560], P('group', 'fsdp'), may hold values from -6 to 6
- kv_inner: bfloat16 [2, 5120, 1024], P('group', 'fsdp'), may hold values from -6 to 6
- kv_outer: float32 [5120, 1024], P('fsdp'), may hold values from -6 to 6
- momentum: float32 [5120, 1024], P('fsdp'), may hold values from -2 to 2
Outputs:
- blended: bfloat16 [2, 5120, 1024], P('group', 'fsdp')
- outer_new: float32 [5120, 1024], P('fsdp')
- momentum_new: float32 [5120, 1024], P('fsdp')
The draws below stay inside these ranges and needn't reach their ends.
All inputs are finite; a program needn't handle non-finite values. Where the reference program divides by a largest or mean magnitude, that divisor is 1e-20 or more.
Results may differ from the reference program's by a relative error of at most 0.025.
The reference program's roundings to bfloat16 on the way (of `rows_in`, `kv_rows`, `kv_grad`, `scales` and `coded`) count: a program that leaves them out, or rounds other values in their place, can miss the bound.
Values may be sent and summed in bfloat16 or wider, within the bound.
No kernel may reach another device: no remote copies, remote signals or barrier semaphores. Data moves between devices by JAX's collectives and lax.ppermute only.
A program may use at most 128 MiB of HBM per device.

```python
import math
import jax
import jax.numpy as jnp
from jax import lax

D = 5120
HD = 128
SEQ = 256
QBLOCK = 128
SEQS_DEV = 2
SEQS = 32
QW = 2560
KVC = 1024
N_GROUP = 2


def draw_hidden(key, part):
    first, second = jax.random.split(key)
    third = jax.random.fold_in(key, 3)
    shape = (N_GROUP, SEQS, SEQ, D)
    row_scale = jnp.exp(jax.random.uniform(second, (N_GROUP, SEQS, SEQ, 1), jnp.float32, 0.0, math.log(10.0)))
    col_scale = jnp.exp(jax.random.uniform(third, (D,), jnp.float32, 0.0, math.log(10.0)))
    values = jnp.clip(jax.random.normal(first, shape, jnp.float32), -6.0, 6.0) * (row_scale * col_scale)
    return jnp.clip(values, -600.0, 600.0).astype(jnp.bfloat16)


def draw_queries(key, part):
    first = jax.random.fold_in(key, 0)
    shape = (N_GROUP, SEQS, SEQ, QW)
    base = jnp.clip(jax.random.normal(first, shape, jnp.float32), -6.0, 6.0)
    return jnp.clip(base, -800.0, 800.0).astype(jnp.bfloat16)


def level_of(stream_key, dims, shards, least, largest):
    factor_of = 1.0
    for axis_at, blocks in shards:
        heights = jax.random.uniform(jax.random.fold_in(jax.random.fold_in(stream_key, 6), axis_at), (blocks,), jnp.float32, least / len(shards), largest / len(shards))
        factor_of = factor_of * jnp.repeat(jnp.exp(heights), dims[axis_at] // blocks).reshape((-1,) + (1,) * (len(dims) - 1 - axis_at))
    return factor_of


def gaussian(own_key, shape, width, reach, cuts=(), held_as=jnp.bfloat16):
    drawn = jax.random.normal(own_key, shape, jnp.float32) * width
    if len(cuts) > 0:
        drawn = level_of(own_key, shape, cuts, -0.22, 0.18) * drawn
    return jnp.clip(drawn, min=-reach, max=reach).astype(held_as)


def setup_inputs(seed: int = 0) -> dict:
    key_list = jax.random.split(jax.random.key(seed), 8)
    hidden = draw_hidden(jax.random.fold_in(key_list[7], 71), 0)
    norm_gain = jnp.clip(1.0 + 0.18 * jax.random.normal(key_list[1], (D,), jnp.float32), 0.1, 1.9)
    queries = draw_queries(jax.random.fold_in(key_list[7], 71), 0)
    out_grad = gaussian(key_list[3], (N_GROUP, SEQS, SEQ, QW), 1.0, 6.0, ((0, 2), (1, 16)))
    kv_inner = gaussian(key_list[4], (N_GROUP, D, KVC), 1.0, 6.0, ((0, 2), (1, 16)))
    kv_outer = gaussian(key_list[5], (D, KVC), 1.0, 6.0, ((0, 16),), jnp.float32)
    momentum = gaussian(key_list[6], (D, KVC), 0.3, 2.0, ((0, 16),), jnp.float32)
    return dict(hidden=hidden, norm_gain=norm_gain, queries=queries, out_grad=out_grad, kv_inner=kv_inner, kv_outer=kv_outer, momentum=momentum)


inner_rate = 0.25
outer_rate = 0.7
momentum_decay = 0.9
blend_share = 0.5
norm_eps = 1e-06
scale_eps = 1e-06

def normed_rows(hidden_rows, norm_gain):
    looked = hidden_rows.reshape(-1, hidden_rows.shape[-1]).astype(jnp.float32)
    mean_sq = lax.optimization_barrier(jnp.mean(looked * looked, axis=-1, keepdims=True))
    return (looked * lax.rsqrt(mean_sq + norm_eps) * norm_gain).astype(jnp.bfloat16)

def attend(queries, kv_rows):
    seq_count, length, query_width = queries.shape
    kv_width = kv_rows.shape[-1] // 2
    kv_heads = kv_width // HD
    repeat = query_width // (kv_heads * HD)
    query_h = queries.reshape(seq_count, length, kv_heads, repeat, HD)
    key_h = kv_rows[..., :kv_width].reshape(seq_count, length, kv_heads, HD)
    value_h = kv_rows[..., kv_width:].reshape(seq_count, length, kv_heads, HD)
    scores = jnp.einsum('slgrd,smgd->sgrlm', query_h, key_h, preferred_element_type=jnp.float32) * HD ** (-0.5)
    places = jnp.arange(length)
    causal = places[None, :] <= places[:, None]
    scores = jnp.where(causal, scores, -1e+30)
    highest = lax.stop_gradient(lax.optimization_barrier(jnp.max(scores, axis=-1, keepdims=True)))
    exp_scores = jnp.exp(scores - highest)
    prob_rows = (exp_scores / lax.optimization_barrier(jnp.sum(exp_scores, axis=-1, keepdims=True))).astype(jnp.bfloat16)
    mixed_out = jnp.einsum('sgrlm,smgd->slgrd', prob_rows, value_h, preferred_element_type=jnp.float32)
    return mixed_out.reshape(seq_count, length, query_width)

def kv_grads(queries, kv_rows, out_grad):

    def loss_part(kv_value):
        return attend(queries, kv_value)
    _, pullback = jax.vjp(loss_part, kv_rows)
    return pullback(out_grad.astype(jnp.float32))[0]

def quantize(delta):
    row_count = delta.shape[0]
    shaped = delta.reshape(row_count, -1, QBLOCK)
    scales = (lax.optimization_barrier(jnp.max(jnp.abs(shaped), axis=-1)) + scale_eps).astype(jnp.bfloat16)
    coded = (shaped / scales.astype(jnp.float32)[..., None]).astype(jnp.bfloat16)
    return (coded.reshape(row_count, -1), scales)

def dequantize(coded, scales):
    row_count = coded.shape[0]
    shaped = coded.reshape(row_count, scales.shape[1], -1).astype(jnp.float32)
    return (shaped * scales.astype(jnp.float32)[..., None]).reshape(row_count, -1)

def reference(hidden, norm_gain, queries, out_grad, kv_inner, kv_outer, momentum):
    inv_root = D ** (-0.5)
    groups = kv_inner.shape[0]
    seq_count = hidden.shape[1]
    block_count = seq_count // SEQS_DEV
    fresh_list = []
    totals = jnp.zeros(kv_outer.shape, kv_outer.dtype)
    for group_idx in range(groups):
        rows_in = normed_rows(hidden[group_idx], norm_gain)
        kv_rows = (jnp.dot(rows_in, kv_inner[group_idx], preferred_element_type=jnp.float32) * inv_root).astype(jnp.bfloat16)
        kv_blocks = kv_rows.reshape(block_count, SEQS_DEV, SEQ, kv_rows.shape[-1])
        query_blocks = queries[group_idx].reshape(block_count, SEQS_DEV, SEQ, queries.shape[-1])
        cotan_blocks = out_grad[group_idx].reshape(block_count, SEQS_DEV, SEQ, out_grad.shape[-1])
        kv_grad = lax.map(lambda triple: kv_grads(triple[0], triple[1], triple[2]), (query_blocks, kv_blocks, cotan_blocks))
        grad_blocks = kv_grad.reshape(block_count, SEQS_DEV * SEQ, kv_rows.shape[-1])
        row_blocks = rows_in.reshape(block_count, SEQS_DEV * SEQ, rows_in.shape[-1])

        def add_block(total, pair):
            partial_sum = lax.dot_general(pair[0], pair[1], (((0,), (0,)), ((), ())), preferred_element_type=jnp.float32) * inv_root
            partial_sum = lax.optimization_barrier(partial_sum.astype(jnp.bfloat16))
            return (total + partial_sum.astype(total.dtype), None)
        gradient, _ = lax.scan(add_block, jnp.zeros(kv_outer.shape, kv_outer.dtype), (row_blocks, grad_blocks))
        fresh = kv_inner[group_idx].astype(jnp.float32) - inner_rate * gradient
        fresh_list.append(fresh)
        coded, scales = quantize(kv_outer - fresh)
        totals = totals + dequantize(coded, scales)
    average = totals / groups
    momentum_new = momentum_decay * momentum + average
    outer_new = kv_outer - outer_rate * (momentum_decay * momentum_new + average)
    blended = jnp.stack([(blend_share * fresh + (1.0 - blend_share) * outer_new).astype(jnp.bfloat16) for fresh in fresh_list])
    return (blended, outer_new, momentum_new)
```

```python
import functools

import jax
import jax.numpy as jnp
import numpy as np
from jax import lax
from jax.experimental import pallas as pl
from jax.experimental.pallas import tpu as pltpu
from jax.sharding import PartitionSpec as P

HD = 128

inner_rate = 0.25
outer_rate = 0.7
momentum_decay = 0.9
blend_share = 0.5
norm_eps = 1e-06
scale_eps = 1e-06

F32 = jnp.float32
BF16 = jnp.bfloat16
VMEM_LIMIT = 56 * 1024 * 1024
SCALE_ROWS = 16


def ring_order(count):
    return list(range(0, count, 2)) + list(range(1, count, 2))[::-1]


def call(body, out_shape, in_specs, out_specs, grid=(1,), scratch=(), flops=0, moved=0, name=None):
    return pl.pallas_call(
        body,
        out_shape=out_shape,
        grid_spec=pltpu.PrefetchScalarGridSpec(
            num_scalar_prefetch=1,
            grid=grid,
            in_specs=in_specs,
            out_specs=out_specs,
            scratch_shapes=list(scratch),
        ),
        compiler_params=pltpu.CompilerParams(
            vmem_limit_bytes=VMEM_LIMIT, dimension_semantics=("arbitrary",) * len(grid)
        ),
        cost_estimate=pl.CostEstimate(flops=int(flops), bytes_accessed=int(moved), transcendentals=0),
        name=name,
    )


def whole(shape):
    zeros = (0,) * len(shape)
    return pl.BlockSpec(shape, lambda i, s: zeros)


def dot_nn(a, b):
    return lax.dot_general(a, b, (((1,), (0,)), ((), ())), preferred_element_type=F32)


def dot_nt(a, b):
    return lax.dot_general(a, b, (((1,), (1,)), ((), ())), preferred_element_type=F32)


def dot_tn(a, b):
    return lax.dot_general(a, b, (((0,), (0,)), ((), ())), preferred_element_type=F32)


def norm_rows(scalars, hidden_rows, norm_gain, chips):
    tokens, width = hidden_rows.shape
    part = width // chips
    tile = 128

    def body(s, x_ref, g_ref, o_ref):
        total = jnp.zeros((tile, 1), F32)
        for b in range(chips):
            x = x_ref[:, b * part : (b + 1) * part].astype(F32)
            total = total + jnp.sum(x * x, axis=-1, keepdims=True)
        factor = lax.rsqrt(total * (1.0 / width) + norm_eps)
        for b in range(chips):
            x = x_ref[:, b * part : (b + 1) * part].astype(F32)
            o_ref[b] = (x * factor * g_ref[:, b * part : (b + 1) * part]).astype(BF16)

    return call(
        body,
        jax.ShapeDtypeStruct((chips, tokens, part), BF16),
        [pl.BlockSpec((tile, width), lambda i, s: (i, 0)), whole((1, width))],
        pl.BlockSpec((chips, tile, part), lambda i, s: (0, i, 0)),
        grid=(tokens // tile,),
        flops=tokens * width * 6,
        moved=tokens * width * 4,
        name="norm",
    )(scalars, hidden_rows, norm_gain.reshape(1, width))


def columns_of(core, head, kv, heads, kv_width):
    return pl.multiple_of(kv * kv_width + (core * heads + head) * HD, HD)


def pick_columns(scalars, weight, heads, name):
    rows, cols = weight.shape

    def body(s, w_ref, o_ref):
        other = 1 - s[0]
        for h in range(heads):
            for kv in range(2):
                at = (h * 2 + kv) * HD
                o_ref[:, at : at + HD] = w_ref[:, pl.ds(columns_of(other, h, kv, heads, cols // 2), HD)]

    return call(
        body,
        jax.ShapeDtypeStruct((rows, cols // 2), weight.dtype),
        [whole((rows, cols))],
        whole((rows, cols // 2)),
        moved=rows * cols * 3,
        name=name,
    )(scalars, weight)


def own_blocks(scalars, weight, received, heads):
    rows, cols = weight.shape

    def body(s, w_ref, r_ref, *o_refs):
        core = s[0]
        mine = pl.multiple_of(core * rows, 16)
        theirs = pl.multiple_of((1 - core) * rows, 16)
        for h in range(heads):
            for kv in range(2):
                at = (h * 2 + kv) * HD
                o_refs[h][pl.ds(mine, rows), kv * HD : (kv + 1) * HD] = w_ref[
                    :, pl.ds(columns_of(core, h, kv, heads, cols // 2), HD)
                ]
                o_refs[h][pl.ds(theirs, rows), kv * HD : (kv + 1) * HD] = r_ref[:, at : at + HD]

    shape = (2 * rows, 2 * HD)
    return call(
        body,
        [jax.ShapeDtypeStruct(shape, weight.dtype)] * heads,
        [whole((rows, cols)), whole((rows, cols // 2))],
        [whole(shape)] * heads,
        moved=rows * cols * 5,
        name="own_blocks",
    )(scalars, weight, received)


def start_deltas(scalars, blocks, outer, received, heads):
    rows, cols = outer.shape

    def body(s, o_ref, r_ref, *refs):
        core = s[0]
        for h in range(heads):
            block_ref, out_ref = refs[h], refs[heads + h]
            for kv in range(2):
                at = (h * 2 + kv) * HD
                mine = o_ref[:, pl.ds(columns_of(core, h, kv, heads, cols // 2), HD)]
                theirs = r_ref[:, at : at + HD]
                first = jnp.where(core == 0, mine, theirs)
                second = jnp.where(core == 0, theirs, mine)
                both = jnp.concatenate([first, second], axis=0)
                both = both - block_ref[:, kv * HD : (kv + 1) * HD].astype(F32)
                out_ref[kv * HD : (kv + 1) * HD, :] = both.T

    return call(
        body,
        [jax.ShapeDtypeStruct((2 * HD, 2 * rows), F32)] * heads,
        [whole((rows, cols)), whole((rows, cols // 2))] + [whole((2 * rows, 2 * HD))] * heads,
        [whole((2 * HD, 2 * rows))] * heads,
        moved=rows * cols * 14,
        name="start_deltas",
    )(scalars, outer, received, *blocks)


def attention_grads(scalars, rows_mine, rows_other, blocks, halves, queries, queries_other, out_grad, out_grad_other, head, heads):
    chips, tokens, part = rows_mine.shape
    seqs, length, query_width = queries.shape
    repeat = query_width // (2 * heads * HD)
    inv_root = (chips * part) ** (-0.5)
    far = chips // 2
    half = length // 2
    places = [k for k in range(chips) if k != far]

    def body(s, a_ref, b_ref, qa_ref, qb_ref, ga_ref, gb_ref, *refs):
        block_refs = refs[: len(places)]
        half_refs = refs[len(places) : len(places) + 2]
        out_ref = refs[len(places) + 2]
        far_ref = refs[len(places) + 3]
        step = pl.program_id(0)

        @pl.when(step == 0)
        def _():
            far_ref[: part // 2, :] = half_refs[0][...]
            far_ref[part // 2 :, :] = half_refs[1][...]

        def work(x_ref, q_ref, g_ref):
            acc = dot_nn(x_ref[s[1 + far]], far_ref[...])
            for ref, k in zip(block_refs, places):
                acc = acc + dot_nn(x_ref[s[1 + k]], ref[...])
            kv = (acc * inv_root).astype(BF16)
            keys, values = kv[:, :HD], kv[:, HD:]
            key_grad = jnp.zeros((HD, length), F32)
            value_grad = jnp.zeros((HD, length), F32)
            for r in range(repeat):
                q_all = q_ref[0, :, r * HD : (r + 1) * HD]
                g_all = g_ref[0, :, r * HD : (r + 1) * HD]
                d_parts, p_parts = [], []
                for t in range(2):
                    cols = (t + 1) * half
                    q = q_all[t * half : (t + 1) * half]
                    g = g_all[t * half : (t + 1) * half]
                    scores = dot_nt(q, keys[:cols]) * HD ** (-0.5)
                    spot = lax.broadcasted_iota(jnp.int32, (half, cols), 0) + t * half
                    causal = lax.broadcasted_iota(jnp.int32, (half, cols), 1) <= spot
                    scores = jnp.where(causal, scores, -1e30)
                    highest = jnp.max(scores, axis=-1, keepdims=True)
                    exps = jnp.exp(scores - highest)
                    prob = exps * (1.0 / jnp.sum(exps, axis=-1, keepdims=True))
                    prob_grad = dot_nt(g, values[:cols]).astype(BF16).astype(F32)
                    weighted = prob * prob_grad
                    mean = jnp.sum(weighted, axis=-1, keepdims=True)
                    d_part = ((weighted - prob * mean) * HD ** (-0.5)).astype(BF16)
                    p_part = prob.astype(BF16)
                    if t == 0:
                        d_part = jnp.concatenate([d_part, jnp.zeros((half, length - cols), BF16)], axis=1)
                        p_part = jnp.concatenate([p_part, jnp.zeros((half, length - cols), BF16)], axis=1)
                    d_parts.append(d_part)
                    p_parts.append(p_part)
                key_grad = key_grad + dot_tn(q_all, jnp.concatenate(d_parts, axis=0))
                value_grad = value_grad + dot_tn(g_all, jnp.concatenate(p_parts, axis=0))
            out_ref[:HD, :] = key_grad.astype(BF16)
            out_ref[HD:, :] = value_grad.astype(BF16)

        @pl.when(step < seqs)
        def _():
            work(a_ref, qa_ref, ga_ref)

        @pl.when(step >= seqs)
        def _():
            work(b_ref, qb_ref, gb_ref)

    first = lambda i: jnp.minimum(i, seqs - 1)
    second = lambda i: jnp.maximum(i - seqs, 0)
    rows_spec = lambda pick: pl.BlockSpec((chips, length, part), lambda i, s: (0, pick(i), 0))
    mine_spec = pl.BlockSpec((1, length, repeat * HD), lambda i, s: (first(i), 0, s[0] * heads + head))
    other_spec = pl.BlockSpec((1, length, repeat * HD), lambda i, s: (second(i), 0, head))
    block = whole((part, 2 * HD))
    half_block = whole((part // 2, 2 * HD))
    work_flops = 2 * tokens * chips * part * 2 * HD * 2 + 2 * seqs * repeat * length * length * HD * 8 * 2
    return call(
        body,
        jax.ShapeDtypeStruct((2 * HD, 2 * tokens), BF16),
        [rows_spec(first), rows_spec(second), mine_spec, other_spec, mine_spec, other_spec]
        + [block] * len(places)
        + [half_block] * 2,
        pl.BlockSpec((2 * HD, length), lambda i, s: (0, i)),
        grid=(2 * seqs,),
        scratch=[pltpu.VMEM((part, 2 * HD), BF16)],
        flops=work_flops,
        moved=2 * tokens * chips * part * 2,
        name=f"attend_{head}",
    )(
        scalars, rows_mine, rows_other, queries, queries_other, out_grad, out_grad_other,
        *[blocks[k] for k in places], *halves,
    )


def far_partials(scalars, kv_grad, rows_mine, rows_other, name):
    chips, tokens, part = rows_mine.shape
    inv_root = (chips * part) ** (-0.5)
    far = chips // 2

    def body(s, k_ref, a_ref, b_ref, up_ref, down_ref):
        total = dot_nn(k_ref[:, :tokens], a_ref[0]) + dot_nn(k_ref[:, tokens:], b_ref[0])
        total = total * inv_root
        up_ref[...] = total[:HD].astype(BF16)
        down_ref[...] = total[HD:].astype(BF16)

    rows_spec = pl.BlockSpec((1, tokens, part), lambda i, s: (s[1 + far], 0, 0))
    shape = (HD, part)
    return call(
        body,
        [jax.ShapeDtypeStruct(shape, BF16)] * 2,
        [whole(kv_grad.shape), rows_spec, rows_spec],
        [whole(shape)] * 2,
        flops=2 * 2 * tokens * part * 2 * HD,
        moved=2 * tokens * part * 2,
        name=name,
    )(scalars, kv_grad, rows_mine, rows_other)


def near_partials(scalars, kv_grad, rows_mine, rows_other, up, down, distance, name):
    chips, tokens, part = rows_mine.shape
    inv_root = (chips * part) ** (-0.5)
    is_half = up.shape[0] == HD

    def body(s, k_ref, a_ref, b_ref, ui_ref, di_ref, up_ref, down_ref):
        step = pl.program_id(0)
        total = dot_nn(k_ref[:, :tokens], a_ref[0]) + dot_nn(k_ref[:, tokens:], b_ref[0])
        total = total * inv_root

        @pl.when(step == 0)
        def _():
            if is_half:
                up_ref[:HD, :] = (total[:HD] + ui_ref[...].astype(F32)).astype(BF16)
                up_ref[HD:, :] = total[HD:].astype(BF16)
            else:
                up_ref[...] = (total + ui_ref[...].astype(F32)).astype(BF16)

        @pl.when(step == 1)
        def _():
            if is_half:
                down_ref[:HD, :] = total[:HD].astype(BF16)
                down_ref[HD:, :] = (total[HD:] + di_ref[...].astype(F32)).astype(BF16)
            else:
                down_ref[...] = (total + di_ref[...].astype(F32)).astype(BF16)

    rows_spec = pl.BlockSpec(
        (1, tokens, part), lambda i, s: (jnp.where(i == 0, s[1 + distance], s[1 + chips - distance]), 0, 0)
    )
    shape = (2 * HD, part)
    return call(
        body,
        [jax.ShapeDtypeStruct(shape, BF16)] * 2,
        [whole(kv_grad.shape), rows_spec, rows_spec, whole(up.shape), whole(down.shape)],
        [whole(shape)] * 2,
        grid=(2,),
        flops=2 * 2 * 2 * tokens * part * 2 * HD,
        moved=2 * 2 * tokens * part * 2,
        name=name,
    )(scalars, kv_grad, rows_mine, rows_other, up, down)


def split_packs(values):
    deep = values.shape[0] // 2
    rows = values.shape[1] // 2
    return [
        jnp.concatenate([values[:deep, k * rows : (k + 1) * rows], values[deep:, k * rows : (k + 1) * rows]], axis=1)
        for k in range(2)
    ]


def code_deltas(scalars, kv_grad, rows_mine, rows_other, up, down, delta_start, name):
    chips, tokens, part = rows_mine.shape
    inv_root = (chips * part) ** (-0.5)

    def body(s, k_ref, a_ref, b_ref, ui_ref, di_ref, d_ref, own_ref, core_ref, y_ref, far_ref):
        core = s[0]
        total = dot_nn(k_ref[:, :tokens], a_ref[0]) + dot_nn(k_ref[:, tokens:], b_ref[0])
        total = total * inv_root + ui_ref[...].astype(F32) + di_ref[...].astype(F32)
        delta = d_ref[...] + inner_rate * total
        scales, coded = [], []
        for kv in range(2):
            piece = delta[kv * HD : (kv + 1) * HD]
            scale = (jnp.max(jnp.abs(piece), axis=0, keepdims=True) + scale_eps).astype(BF16).astype(F32)
            scales.append(scale)
            coded.append(piece / scale)
        grads = split_packs(total)
        codes = split_packs(jnp.concatenate(coded, axis=0))
        levels = split_packs(jnp.concatenate(scales, axis=0))
        for mine, wide_ref, thin_ref in ((True, own_ref, y_ref), (False, core_ref, far_ref)):
            first = (core == 0) if mine else (core == 1)
            grad = jnp.where(first, grads[0], grads[1]).astype(BF16)
            code = jnp.where(first, codes[0], codes[1]).astype(BF16)
            level = jnp.where(first, levels[0], levels[1])
            level = jnp.broadcast_to(level, (SCALE_ROWS, part)).astype(BF16)
            wide_ref[:HD, :] = code
            wide_ref[HD : HD + SCALE_ROWS, :] = level
            wide_ref[HD + SCALE_ROWS :, :] = grad
            thin_ref[:HD, :] = code
            thin_ref[HD:, :] = level

    rows_spec = pl.BlockSpec((1, tokens, part), lambda i, s: (s[1], 0, 0))
    wide, thin = (2 * HD + SCALE_ROWS, part), (HD + SCALE_ROWS, part)
    return call(
        body,
        [jax.ShapeDtypeStruct(shape, BF16) for shape in (wide, wide, thin, thin)],
        [whole(kv_grad.shape), rows_spec, rows_spec, whole(up.shape), whole(down.shape), whole(delta_start.shape)],
        [whole(wide), whole(wide), whole(thin), whole(thin)],
        flops=2 * 2 * tokens * part * 2 * HD,
        moved=2 * tokens * part * 2,
        name=name,
    )(scalars, kv_grad, rows_mine, rows_other, up, down, delta_start)


def finish(scalars, weight, outer, momentum, grads, codes, heads):
    rows, cols = weight.shape
    groups = len(codes[0][0])
    packs = []
    for h in range(heads):
        for side in range(2):
            packs.append(grads[h][side])
            packs.extend(codes[h][side])

    def body(s, w_ref, k_ref, m_ref, *refs):
        pack_refs = refs[: len(packs)]
        blend_ref, outer_ref, moment_ref = refs[len(packs) :]
        at = 0
        for h in range(heads):
            for side in range(2):
                grad_ref = pack_refs[at]
                code_refs = pack_refs[at + 1 : at + 1 + groups]
                at += 1 + groups
                core = s[0] if side == 0 else 1 - s[0]
                for kv in range(2):
                    lanes = slice(kv * rows, (kv + 1) * rows)
                    grad = grad_ref[HD + SCALE_ROWS :, lanes].astype(F32).T
                    total = jnp.zeros((HD, rows), F32)
                    for ref in code_refs:
                        total = total + ref[:HD, lanes].astype(F32) * ref[HD : HD + 1, lanes].astype(F32)
                    average = (total / groups).T
                    where = pl.ds(columns_of(core, h, kv, heads, cols // 2), HD)
                    fresh = w_ref[:, where].astype(F32) - inner_rate * grad
                    moment = momentum_decay * m_ref[:, where] + average
                    stepped = k_ref[:, where] - outer_rate * (momentum_decay * moment + average)
                    moment_ref[:, where] = moment
                    outer_ref[:, where] = stepped
                    blend_ref[:, where] = (blend_share * fresh + (1.0 - blend_share) * stepped).astype(BF16)

    full = whole((rows, cols))
    return call(
        body,
        [
            jax.ShapeDtypeStruct((rows, cols), BF16),
            jax.ShapeDtypeStruct((rows, cols), F32),
            jax.ShapeDtypeStruct((rows, cols), F32),
        ],
        [full] * 3 + [whole(p.shape) for p in packs],
        [full] * 3,
        moved=rows * cols * 24,
        name="finish",
    )(scalars, weight, outer, momentum, *packs)


def local(hidden, norm_gain, queries, out_grad, kv_inner, kv_outer, momentum):
    count = lax.axis_size("fsdp")
    groups = lax.axis_size("group")
    index = lax.axis_index("fsdp")
    group = lax.axis_index("group")
    chips = count // 2
    far = chips // 2
    ring = ring_order(chips)
    place = {chip: at for at, chip in enumerate(ring)}
    walks = np.array([[ring[(place[j] + k) % chips] for k in range(chips)] for j in range(chips)], np.int32)
    core = index % 2
    scalars = jnp.concatenate([core[None].astype(jnp.int32), jnp.asarray(walks)[index // 2]])

    def around(shift):
        return [(2 * j + c, 2 * ring[(place[j] + shift) % chips] + c) for j in range(chips) for c in range(2)]

    up = functools.partial(lax.ppermute, axis_name="fsdp", perm=around(1))
    down = functools.partial(lax.ppermute, axis_name="fsdp", perm=around(-1))
    swap = functools.partial(lax.ppermute, axis_name="fsdp", perm=[(i, i ^ 1) for i in range(count)])

    def across(values, shift, flip):
        pairs = [
            (g * count + i, (g + shift) % groups * count + (i ^ flip)) for g in range(groups) for i in range(count)
        ]
        return lax.ppermute(values, ("group", "fsdp"), pairs)

    weight = kv_inner[0]
    rows, cols = weight.shape
    heads = cols // 2 // HD // 2
    seqs, length, width = hidden.shape[1:]
    half_width = queries.shape[-1] // 2

    received = swap(pick_columns(scalars, weight, heads, "pick_inner"))
    own = own_blocks(scalars, weight, received, heads)

    blocks = [{0: own[h]} for h in range(heads)]
    halves = [None] * heads
    part = 2 * rows
    ups, downs = list(own), list(own)
    for step in range(1, far + 1):
        for h in range(heads):
            if step < far:
                ups[h], downs[h] = up(ups[h]), down(downs[h])
                blocks[h][chips - step], blocks[h][step] = ups[h], downs[h]
            else:
                halves[h] = (up(ups[h][: part // 2]), down(downs[h][part // 2 :]))

    rows_mine = norm_rows(scalars, hidden.reshape(seqs * length, width), norm_gain, chips)
    rows_other = swap(rows_mine)
    at = ((1 - core) * half_width).astype(jnp.int32)
    queries_other = swap(lax.dynamic_slice_in_dim(queries[0], at, half_width, axis=2))
    out_grad_other = swap(lax.dynamic_slice_in_dim(out_grad[0], at, half_width, axis=2))
    outer_other = swap(pick_columns(scalars, kv_outer, heads, "pick_outer"))
    deltas = start_deltas(scalars, own, kv_outer, outer_other, heads)

    kv_grad = [
        attention_grads(
            scalars, rows_mine, rows_other, blocks[h], halves[h],
            queries[0], queries_other, out_grad[0], out_grad_other, h, heads,
        )
        for h in range(heads)
    ]

    grads, codes = [], []
    for h in range(heads):
        going_up, going_down = far_partials(scalars, kv_grad[h], rows_mine, rows_other, f"far_{h}")
        for distance in range(far - 1, 0, -1):
            going_up, going_down = near_partials(
                scalars, kv_grad[h], rows_mine, rows_other, up(going_up), down(going_down), distance, f"near_{h}_{distance}"
            )
        own_pack, core_pack, thin_own, thin_core = code_deltas(
            scalars, kv_grad[h], rows_mine, rows_other, up(going_up), down(going_down), deltas[h], f"code_{h}"
        )
        from_core = swap(core_pack)
        mine = [own_pack] + [across(thin_own, k, 0) for k in range(1, groups)]
        theirs = [from_core] + [across(thin_core, k, 1) for k in range(1, groups)]
        if groups > 2:
            deep = HD + SCALE_ROWS
            ordered = []
            for packs in (mine, theirs):
                stacked = jnp.stack([p[:deep] for p in packs])
                ordered.append([stacked[(group - g) % groups] for g in range(groups)])
            mine_codes, their_codes = ordered
        else:
            mine_codes, their_codes = mine, theirs
        grads.append((own_pack, from_core))
        codes.append((mine_codes, their_codes))

    blended, outer_new, momentum_new = finish(scalars, weight, kv_outer, momentum, grads, codes, heads)
    return (blended[None], outer_new, momentum_new)


def solution(mesh):
    in_specs = (
        P("group", "fsdp", None, None),
        P(),
        P("group", "fsdp", None, None),
        P("group", "fsdp", None, None),
        P("group", "fsdp", None),
        P("fsdp", None),
        P("fsdp", None),
    )
    out_specs = (P("group", "fsdp", None), P("fsdp", None), P("fsdp", None))
    return jax.shard_map(local, mesh=mesh, in_specs=in_specs, out_specs=out_specs, check_vma=False)
```

```python
import functools

import jax
import jax.numpy as jnp
import numpy as np
from jax import lax
from jax.experimental import pallas as pl
from jax.experimental.pallas import tpu as pltpu
from jax.sharding import PartitionSpec as P

HD = 128

inner_rate = 0.25
outer_rate = 0.7
momentum_decay = 0.9
blend_share = 0.5
norm_eps = 1e-06
scale_eps = 1e-06

F32 = jnp.float32
BF16 = jnp.bfloat16
VMEM_LIMIT = 62 * 1024 * 1024
SCALE_ROWS = 16


def ring_order(count):
    return list(range(0, count, 2)) + list(range(1, count, 2))[::-1]


def call(body, out_shape, in_specs, out_specs, grid=(1,), scratch=(), flops=0, moved=0, aliases=None, name=None):
    return pl.pallas_call(
        body,
        out_shape=out_shape,
        grid_spec=pltpu.PrefetchScalarGridSpec(
            num_scalar_prefetch=1,
            grid=grid,
            in_specs=in_specs,
            out_specs=out_specs,
            scratch_shapes=list(scratch),
        ),
        compiler_params=pltpu.CompilerParams(
            vmem_limit_bytes=VMEM_LIMIT, dimension_semantics=("arbitrary",) * len(grid)
        ),
        cost_estimate=pl.CostEstimate(flops=int(flops), bytes_accessed=int(moved), transcendentals=0),
        input_output_aliases=aliases or {},
        name=name,
    )


def whole(shape):
    zeros = (0,) * len(shape)
    return pl.BlockSpec(shape, lambda i, s: zeros)


def dot_nn(a, b):
    return lax.dot_general(a, b, (((1,), (0,)), ((), ())), preferred_element_type=F32)


def dot_nt(a, b):
    return lax.dot_general(a, b, (((1,), (1,)), ((), ())), preferred_element_type=F32)


def dot_tn(a, b):
    return lax.dot_general(a, b, (((0,), (0,)), ((), ())), preferred_element_type=F32)


def norm_rows(scalars, hidden_rows, norm_gain, chips):
    tokens, width = hidden_rows.shape
    part = width // chips
    tile = 128

    def body(s, x_ref, g_ref, o_ref):
        total = jnp.zeros((tile, 1), F32)
        for b in range(chips):
            x = x_ref[:, b * part : (b + 1) * part].astype(F32)
            total = total + jnp.sum(x * x, axis=-1, keepdims=True)
        factor = lax.rsqrt(total * (1.0 / width) + norm_eps)
        for b in range(chips):
            x = x_ref[:, b * part : (b + 1) * part].astype(F32)
            o_ref[b] = (x * factor * g_ref[:, b * part : (b + 1) * part]).astype(BF16)

    return call(
        body,
        jax.ShapeDtypeStruct((chips, tokens, part), BF16),
        [pl.BlockSpec((tile, width), lambda i, s: (i, 0)), whole((1, width))],
        pl.BlockSpec((chips, tile, part), lambda i, s: (0, i, 0)),
        grid=(tokens // tile,),
        flops=tokens * width * 6,
        moved=tokens * width * 4,
        name="norm",
    )(scalars, hidden_rows, norm_gain.reshape(1, width))


def columns_of(core, head, kv, heads, kv_width):
    return pl.multiple_of(kv * kv_width + (core * heads + head) * HD, HD)


def own_blocks(scalars, weight, received, heads):
    rows, cols = weight.shape

    def body(s, w_ref, r_ref, *o_refs):
        core = s[0]
        mine = pl.multiple_of(core * rows, 16)
        theirs = pl.multiple_of((1 - core) * rows, 16)
        for h in range(heads):
            for kv in range(2):
                there = pl.ds(columns_of(core, h, kv, heads, cols // 2), HD)
                lanes = slice(kv * HD, (kv + 1) * HD)
                o_refs[h][pl.ds(mine, rows), lanes] = w_ref[:, there]
                o_refs[h][pl.ds(theirs, rows), lanes] = r_ref[:, there]

    shape = (2 * rows, 2 * HD)
    return call(
        body,
        [jax.ShapeDtypeStruct(shape, weight.dtype)] * heads,
        [whole((rows, cols))] * 2,
        [whole(shape)] * heads,
        moved=rows * cols * 6,
        name="own_blocks",
    )(scalars, weight, received)


def start_deltas(scalars, blocks, outer, received, heads):
    rows, cols = outer.shape

    def body(s, o_ref, r_ref, *refs):
        core = s[0]
        for h in range(heads):
            block_ref, out_ref = refs[h], refs[heads + h]
            for kv in range(2):
                there = pl.ds(columns_of(core, h, kv, heads, cols // 2), HD)
                mine = o_ref[:, there]
                theirs = r_ref[:, there]
                first = jnp.where(core == 0, mine, theirs)
                second = jnp.where(core == 0, theirs, mine)
                both = jnp.concatenate([first, second], axis=0)
                both = both - block_ref[:, kv * HD : (kv + 1) * HD].astype(F32)
                out_ref[kv * HD : (kv + 1) * HD, :] = both.T

    return call(
        body,
        [jax.ShapeDtypeStruct((2 * HD, 2 * rows), F32)] * heads,
        [whole((rows, cols))] * 2 + [whole((2 * rows, 2 * HD))] * heads,
        [whole((2 * HD, 2 * rows))] * heads,
        moved=rows * cols * 14,
        name="start_deltas",
    )(scalars, outer, received, *blocks)


def project_part(scalars, rows_mine, rows_other, blocks, base, acc, name):
    chips, tokens, part = rows_mine.shape
    count = len(blocks)

    def body(s, a_ref, b_ref, *refs):
        block_refs = refs[:count]
        acc_ref = refs[count] if acc is not None else None
        out_ref, held, sems = refs[-3:]
        copies = []
        for k in range(count):
            for side, ref in enumerate((a_ref, b_ref)):
                copies.append(pltpu.make_async_copy(ref.at[s[1 + base + k]], held.at[k, side], sems.at[k, side]))
        for copy in copies:
            copy.start()
        for k in range(count):
            for side in range(2):
                copies[2 * k + side].wait()
                here = slice(side * tokens, (side + 1) * tokens)
                product = dot_nn(held[k, side], block_refs[k][...])
                if k > 0:
                    product = product + out_ref[here, :]
                elif acc is not None:
                    product = product + acc_ref[here, :]
                out_ref[here, :] = product

    shape = (2 * tokens, 2 * HD)
    any_spec = pl.BlockSpec(memory_space=pl.ANY)
    inputs = [rows_mine, rows_other, *blocks] + ([acc] if acc is not None else [])
    return call(
        body,
        jax.ShapeDtypeStruct(shape, F32),
        [any_spec, any_spec] + [whole(b.shape) for b in blocks] + ([whole(shape)] if acc is not None else []),
        whole(shape),
        scratch=[pltpu.VMEM((count, 2, tokens, part), BF16), pltpu.SemaphoreType.DMA((count, 2))],
        flops=2 * 2 * tokens * part * 2 * HD * count,
        moved=2 * tokens * part * 2 * count,
        name=name,
    )(scalars, *inputs)


def attention_grads(scalars, acc, rows_mine, rows_other, blocks, halves, base, queries, queries_other, out_grad, out_grad_other, head, heads):
    chips, tokens, part = rows_mine.shape
    seqs, length, query_width = queries.shape
    repeat = query_width // (2 * heads * HD)
    inv_root = (chips * part) ** (-0.5)
    half = length // 2
    count = len(blocks)
    last = chips - 1
    two_power = HD ** (-0.5) * 1.4426950408889634

    def body(s, acc_ref, qa_ref, qb_ref, ga_ref, gb_ref, fa_ref, fb_ref, *refs):
        row_refs = (refs[: count + 1], refs[count + 1 : 2 * count + 2])
        refs = refs[2 * count + 2 :]
        block_refs, half_refs = refs[:count], refs[count : count + 2]
        out_ref, up_ref, down_ref, far_ref, grad_ref = refs[count + 2 :]
        step = pl.program_id(0)

        @pl.when(step == 0)
        def _():
            far_ref[: part // 2, :] = half_refs[0][...]
            far_ref[part // 2 :, :] = half_refs[1][...]

        def work(x_refs, q_ref, g_ref):
            total = acc_ref[...]
            for ref, block_ref in zip(x_refs, list(block_refs) + [far_ref]):
                total = total + dot_nn(ref[0], block_ref[...])
            kv = (total * inv_root).astype(BF16)
            keys, values = kv[:, :HD], kv[:, HD:]
            found = []
            for t in range(2):
                cols = (t + 1) * half
                rows_of = slice(t * half, (t + 1) * half)
                q = jnp.concatenate([q_ref[0, rows_of, r * HD : (r + 1) * HD] for r in range(repeat)], axis=0)
                g = jnp.concatenate([g_ref[0, rows_of, r * HD : (r + 1) * HD] for r in range(repeat)], axis=0)
                scores = dot_nt(q, keys[:cols]) * two_power
                spot = lax.broadcasted_iota(jnp.int32, (half, cols), 0) + t * half
                causal = lax.broadcasted_iota(jnp.int32, (half, cols), 1) <= spot
                causal = jnp.concatenate([causal.astype(F32)] * repeat, axis=0) > 0.0
                scores = jnp.where(causal, scores, -1e30)
                highest = jnp.max(scores, axis=-1, keepdims=True)
                exps = jnp.exp2(scores - highest)
                prob = exps * (1.0 / jnp.sum(exps, axis=-1, keepdims=True))
                prob_grad = dot_nt(g, values[:cols]).astype(BF16).astype(F32)
                weighted = prob * prob_grad
                mean = jnp.sum(weighted, axis=-1, keepdims=True)
                score_grad = (weighted - prob * mean).astype(BF16)
                found.append((dot_tn(q, score_grad), dot_tn(g, prob.astype(BF16))))
            for at, factor in ((0, HD ** (-0.5)), (1, 1.0)):
                grad_rows = slice(at * HD, (at + 1) * HD)
                early, late = found[0][at], found[1][at]
                grad = jnp.concatenate([(late[:, :half] + early) * factor, late[:, half:] * factor], axis=1).astype(BF16)
                out_ref[grad_rows, :] = grad
                grad_ref[step, grad_rows, :] = grad

        @pl.when(step < seqs)
        def _():
            work(row_refs[0], qa_ref, ga_ref)

        @pl.when(step >= seqs)
        def _():
            work(row_refs[1], qb_ref, gb_ref)

        @pl.when(step == 2 * seqs - 1)
        def _():
            total = jnp.zeros((2 * HD, part), F32)
            for at in range(seqs):
                here = slice(at * length, (at + 1) * length)
                total = total + dot_nn(grad_ref[at], fa_ref[0, here, :]) + dot_nn(grad_ref[seqs + at], fb_ref[0, here, :])
            total = total * inv_root
            up_ref[...] = total[:HD].astype(BF16)
            down_ref[...] = total[HD:].astype(BF16)

    first = lambda i: jnp.minimum(i, seqs - 1)
    second = lambda i: jnp.maximum(i - seqs, 0)

    def rows_spec(pick, place):
        return pl.BlockSpec((1, length, part), lambda i, s: (s[1 + place], pick(i), 0))

    mine_spec = pl.BlockSpec((1, length, repeat * HD), lambda i, s: (first(i), 0, s[0] * heads + head))
    other_spec = pl.BlockSpec((1, length, repeat * HD), lambda i, s: (second(i), 0, head))
    far_spec = pl.BlockSpec((1, tokens, part), lambda i, s: (s[1 + last], 0, 0))
    places = [base + k for k in range(count)] + [last]
    half_shape = (HD, part)
    work_flops = 2 * tokens * part * 2 * HD * 2 * len(places) + 2 * seqs * repeat * length * length * HD * 8 * 4
    return call(
        body,
        [jax.ShapeDtypeStruct((2 * HD, 2 * tokens), BF16)] + [jax.ShapeDtypeStruct(half_shape, BF16)] * 2,
        [pl.BlockSpec((length, 2 * HD), lambda i, s: (i, 0)), mine_spec, other_spec, mine_spec, other_spec, far_spec, far_spec]
        + [rows_spec(first, p) for p in places]
        + [rows_spec(second, p) for p in places]
        + [whole(b.shape) for b in blocks]
        + [whole(h.shape) for h in halves],
        [pl.BlockSpec((2 * HD, length), lambda i, s: (0, i)), whole(half_shape), whole(half_shape)],
        grid=(2 * seqs,),
        scratch=[pltpu.VMEM((part, 2 * HD), BF16), pltpu.VMEM((2 * seqs, 2 * HD, length), BF16)],
        flops=work_flops,
        moved=2 * tokens * part * 2 * len(places),
        name=f"attend_{head}",
    )(
        scalars, acc, queries, queries_other, out_grad, out_grad_other, rows_mine, rows_other,
        *[rows_mine] * len(places), *[rows_other] * len(places), *blocks, *halves,
    )


def partials(scalars, kv_grad, rows_mine, rows_other, name):
    chips, tokens, part = rows_mine.shape
    inv_root = (chips * part) ** (-0.5)
    count = chips - 1

    def body(s, k_ref, a_ref, b_ref, out_ref, held, done, in_sems, out_sems):
        copies = {}
        for k in reversed(range(count)):
            for side, ref in enumerate((a_ref, b_ref)):
                copies[k, side] = pltpu.make_async_copy(ref.at[s[1 + k]], held.at[k, side], in_sems.at[k, side])
                copies[k, side].start()
        leaving = []
        for k in reversed(range(count)):
            copies[k, 0].wait()
            copies[k, 1].wait()
            total = dot_nn(k_ref[:, :tokens], held[k, 0]) + dot_nn(k_ref[:, tokens:], held[k, 1])
            done[k] = (total * inv_root).astype(BF16)
            leaving.append(pltpu.make_async_copy(done.at[k], out_ref.at[k], out_sems.at[k]))
            leaving[-1].start()
        for copy in leaving:
            copy.wait()

    any_spec = pl.BlockSpec(memory_space=pl.ANY)
    shape = (count, 2 * HD, part)
    return call(
        body,
        jax.ShapeDtypeStruct(shape, BF16),
        [whole(kv_grad.shape), any_spec, any_spec],
        any_spec,
        scratch=[
            pltpu.VMEM((count, 2, tokens, part), BF16),
            pltpu.VMEM(shape, BF16),
            pltpu.SemaphoreType.DMA((count, 2)),
            pltpu.SemaphoreType.DMA((count,)),
        ],
        flops=2 * 2 * tokens * part * 2 * HD * count,
        moved=2 * tokens * part * 2 * count,
        name=name,
    )(scalars, kv_grad, rows_mine, rows_other)


def add_partials(scalars, own, up, down, distance, name):
    part = own.shape[-1]
    is_half = up.shape[0] == HD
    at = 2 * distance - 1

    def body(s, ou_ref, od_ref, ui_ref, di_ref, up_ref, down_ref):
        mine_up, mine_down = ou_ref[0].astype(F32), od_ref[0].astype(F32)
        if is_half:
            keys = pl.program_id(0) == 0
            up_ref[...] = jnp.where(keys, mine_up + ui_ref[...].astype(F32), mine_up).astype(BF16)
            down_ref[...] = jnp.where(keys, mine_down, mine_down + di_ref[...].astype(F32)).astype(BF16)
        else:
            up_ref[...] = (mine_up + ui_ref[...].astype(F32)).astype(BF16)
            down_ref[...] = (mine_down + di_ref[...].astype(F32)).astype(BF16)

    block = (HD, part)
    came = whole(block) if is_half else pl.BlockSpec(block, lambda i, s: (i, 0))
    shape = jax.ShapeDtypeStruct((2 * HD, part), BF16)
    return call(
        body,
        [shape] * 2,
        [
            pl.BlockSpec((1, HD, part), lambda i, s: (at, i, 0)),
            pl.BlockSpec((1, HD, part), lambda i, s: (at + 1, i, 0)),
            came,
            came,
        ],
        [pl.BlockSpec(block, lambda i, s: (i, 0))] * 2,
        grid=(2,),
        moved=2 * HD * part * 12,
        name=name,
    )(scalars, own, own, up, down)


def split_packs(values):
    deep = values.shape[0] // 2
    rows = values.shape[1] // 2
    return [
        jnp.concatenate([values[:deep, k * rows : (k + 1) * rows], values[deep:, k * rows : (k + 1) * rows]], axis=1)
        for k in range(2)
    ]


def code_deltas(scalars, own, up, down, delta_start, name):
    part = own.shape[-1]

    def body(s, g_ref, ui_ref, di_ref, d_ref, own_ref, core_ref, y_ref, far_ref):
        core = s[0]
        total = g_ref[0].astype(F32) + ui_ref[...].astype(F32) + di_ref[...].astype(F32)
        delta = d_ref[...] + inner_rate * total
        scales, coded = [], []
        for kv in range(2):
            piece = delta[kv * HD : (kv + 1) * HD]
            scale = (jnp.max(jnp.abs(piece), axis=0, keepdims=True) + scale_eps).astype(BF16).astype(F32)
            scales.append(scale)
            coded.append(piece / scale)
        grads = split_packs(total)
        codes = split_packs(jnp.concatenate(coded, axis=0))
        levels = split_packs(jnp.concatenate(scales, axis=0))
        for mine, wide_ref, thin_ref in ((True, own_ref, y_ref), (False, core_ref, far_ref)):
            first = (core == 0) if mine else (core == 1)
            grad = jnp.where(first, grads[0], grads[1]).astype(BF16)
            code = jnp.where(first, codes[0], codes[1]).astype(BF16)
            level = jnp.where(first, levels[0], levels[1])
            level = jnp.broadcast_to(level, (SCALE_ROWS, part)).astype(BF16)
            wide_ref[:HD, :] = code
            wide_ref[HD : HD + SCALE_ROWS, :] = level
            wide_ref[HD + SCALE_ROWS :, :] = grad
            thin_ref[:HD, :] = code
            thin_ref[HD:, :] = level

    wide, thin = (2 * HD + SCALE_ROWS, part), (HD + SCALE_ROWS, part)
    return call(
        body,
        [jax.ShapeDtypeStruct(shape, BF16) for shape in (wide, wide, thin, thin)],
        [
            pl.BlockSpec((1, 2 * HD, part), lambda i, s: (0, 0, 0)),
            whole(up.shape),
            whole(down.shape),
            whole(delta_start.shape),
        ],
        [whole(wide), whole(wide), whole(thin), whole(thin)],
        moved=2 * HD * part * 16,
        name=name,
    )(scalars, own, up, down, delta_start)


def finish(scalars, weight, outer, momentum, grads, codes, before, head, heads):
    rows, cols = weight.shape
    groups = len(codes[0])
    packs = [*codes[0], grads[0], *codes[1], grads[1]]
    kept = [] if before is None else list(before)

    def body(s, w_ref, k_ref, m_ref, *refs):
        pack_refs = refs[: len(packs)]
        blend_ref, outer_ref, moment_ref = refs[len(packs) + len(kept) :]
        step = pl.program_id(0)
        for side in range(2):
            code_refs = pack_refs[side * (groups + 1) : side * (groups + 1) + groups]
            grad_ref = pack_refs[side * (groups + 1) + groups]
            for kv in range(2):

                @pl.when(step == 2 * side + kv)
                def _():
                    lanes = slice(kv * rows, (kv + 1) * rows)
                    grad = grad_ref[HD + SCALE_ROWS :, lanes].astype(F32).T
                    total = jnp.zeros((HD, rows), F32)
                    for ref in code_refs:
                        total = total + ref[:HD, lanes].astype(F32) * ref[HD : HD + 1, lanes].astype(F32)
                    average = (total / groups).T
                    fresh = w_ref[...].astype(F32) - inner_rate * grad
                    moment = momentum_decay * m_ref[...] + average
                    stepped = k_ref[...] - outer_rate * (momentum_decay * moment + average)
                    moment_ref[...] = moment
                    outer_ref[...] = stepped
                    blend_ref[...] = (blend_share * fresh + (1.0 - blend_share) * stepped).astype(BF16)

    block = pl.BlockSpec(
        (rows, HD), lambda i, s: (0, i % 2 * 2 * heads + jnp.where(i < 2, s[0], 1 - s[0]) * heads + head)
    )
    any_spec = pl.BlockSpec(memory_space=pl.ANY)
    return call(
        body,
        [
            jax.ShapeDtypeStruct((rows, cols), BF16),
            jax.ShapeDtypeStruct((rows, cols), F32),
            jax.ShapeDtypeStruct((rows, cols), F32),
        ],
        [block] * 3 + [whole(p.shape) for p in packs] + [any_spec] * len(kept),
        [block] * 3,
        grid=(4,),
        moved=rows * cols * 12,
        aliases={4 + len(packs) + k: k for k in range(len(kept))},
        name=f"finish_{head}",
    )(scalars, weight, outer, momentum, *packs, *kept)


def local(hidden, norm_gain, queries, out_grad, kv_inner, kv_outer, momentum):
    count = lax.axis_size("fsdp")
    groups = lax.axis_size("group")
    index = lax.axis_index("fsdp")
    group = lax.axis_index("group")
    chips = count // 2
    far = chips // 2
    ring = ring_order(chips)
    place = {chip: at for at, chip in enumerate(ring)}
    order = [0] + [k % chips for step in range(1, far) for k in (step, -step)] + [far]
    walks = np.array([[ring[(place[j] + k) % chips] for k in order] for j in range(chips)], np.int32)
    core = index % 2
    scalars = jnp.concatenate([core[None].astype(jnp.int32), jnp.asarray(walks)[index // 2]])

    def around(shift):
        return [(2 * j + c, 2 * ring[(place[j] + shift) % chips] + c) for j in range(chips) for c in range(2)]

    up = functools.partial(lax.ppermute, axis_name="fsdp", perm=around(1))
    down = functools.partial(lax.ppermute, axis_name="fsdp", perm=around(-1))
    swap = functools.partial(lax.ppermute, axis_name="fsdp", perm=[(i, i ^ 1) for i in range(count)])

    def across(values, shift, flip):
        pairs = [
            (g * count + i, (g + shift) % groups * count + (i ^ flip)) for g in range(groups) for i in range(count)
        ]
        return lax.ppermute(values, ("group", "fsdp"), pairs)

    weight = kv_inner[0]
    rows, cols = weight.shape
    heads = cols // 2 // HD // 2
    seqs, length, width = hidden.shape[1:]
    half_width = queries.shape[-1] // 2
    part = 2 * rows

    own = own_blocks(scalars, weight, swap(weight), heads)
    hidden, queries, out_grad, outer_held, own = lax.optimization_barrier((hidden, queries, out_grad, kv_outer, own))

    blocks = [[own[h]] for h in range(heads)]
    halves = [None] * heads
    ups, downs = list(own), list(own)
    for step in range(1, far + 1):
        for h in range(heads):
            if step < far:
                ups[h], downs[h] = up(ups[h]), down(downs[h])
                blocks[h] += [downs[h], ups[h]]
            else:
                halves[h] = (up(ups[h][: part // 2]), down(downs[h][part // 2 :]))

    rows_mine = norm_rows(scalars, hidden.reshape(seqs * length, width), norm_gain, chips)
    rows_other = swap(rows_mine)
    at = ((1 - core) * half_width).astype(jnp.int32)
    queries_other = swap(lax.dynamic_slice_in_dim(queries[0], at, half_width, axis=2))
    out_grad_other = swap(lax.dynamic_slice_in_dim(out_grad[0], at, half_width, axis=2))
    deltas = start_deltas(scalars, own, outer_held, swap(outer_held), heads)

    kv_grad, far_up, far_down = [None] * heads, [None] * heads, [None] * heads
    accs = [None] * heads
    bounds = [0, 3] + [2 * step + 1 for step in range(2, far - 1)]
    for base, end in zip(bounds, bounds[1:]):
        for h in range(heads):
            accs[h] = project_part(scalars, rows_mine, rows_other, blocks[h][base:end], base, accs[h], f"project_{h}_{base}")
    accs, deltas = lax.optimization_barrier((accs, deltas))
    for h in range(heads):
        kv_grad[h], far_up[h], far_down[h] = attention_grads(
            scalars, accs[h], rows_mine, rows_other, blocks[h][bounds[-1] :], halves[h], bounds[-1],
            queries[0], queries_other, out_grad[0], out_grad_other, h, heads,
        )

    outs = None
    for h in range(heads):
        sums = partials(scalars, kv_grad[h], rows_mine, rows_other, f"partials_{h}")
        going_up, going_down = far_up[h], far_down[h]
        for distance in range(far - 1, 0, -1):
            going_up, going_down = add_partials(
                scalars, sums, up(going_up), down(going_down), distance, f"add_{h}_{distance}"
            )
        own_pack, core_pack, thin_own, thin_core = code_deltas(
            scalars, sums, up(going_up), down(going_down), deltas[h], f"code_{h}"
        )
        from_core = swap(core_pack)
        mine = [own_pack] + [across(thin_own, k, 0) for k in range(1, groups)]
        theirs = [from_core] + [across(thin_core, k, 1) for k in range(1, groups)]
        if groups > 2:
            deep = HD + SCALE_ROWS
            ordered = []
            for packs in (mine, theirs):
                stacked = jnp.stack([p[:deep] for p in packs])
                ordered.append([stacked[(group - g) % groups] for g in range(groups)])
            mine, theirs = ordered
        outs = finish(
            scalars, weight, kv_outer, momentum, (own_pack, from_core), (mine, theirs), outs, h, heads
        )

    blended, outer_new, momentum_new = outs
    return (blended[None], outer_new, momentum_new)


def solution(mesh):
    in_specs = (
        P("group", "fsdp", None, None),
        P(),
        P("group", "fsdp", None, None),
        P("group", "fsdp", None, None),
        P("group", "fsdp", None),
        P("fsdp", None),
        P("fsdp", None),
    )
    out_specs = (P("group", "fsdp", None), P("fsdp", None), P("fsdp", None))
    return jax.shard_map(local, mesh=mesh, in_specs=in_specs, out_specs=out_specs, check_vma=False)
```

```python
import functools

import jax
import jax.numpy as jnp
import numpy as np
from jax import lax
from jax.experimental import pallas as pl
from jax.experimental.pallas import tpu as pltpu
from jax.sharding import PartitionSpec as P

HD = 128

inner_rate = 0.25
outer_rate = 0.7
momentum_decay = 0.9
blend_share = 0.5
norm_eps = 1e-06
scale_eps = 1e-06

F32 = jnp.float32
BF16 = jnp.bfloat16
VMEM_LIMIT = 62 * 1024 * 1024
SCALE_ROWS = 16


def ring_order(count):
    return list(range(0, count, 2)) + list(range(1, count, 2))[::-1]


def call(body, out_shape, in_specs, out_specs, grid=(1,), scratch=(), flops=0, moved=0, aliases=None, name=None):
    return pl.pallas_call(
        body,
        out_shape=out_shape,
        grid_spec=pltpu.PrefetchScalarGridSpec(
            num_scalar_prefetch=1,
            grid=grid,
            in_specs=in_specs,
            out_specs=out_specs,
            scratch_shapes=list(scratch),
        ),
        compiler_params=pltpu.CompilerParams(
            vmem_limit_bytes=VMEM_LIMIT, dimension_semantics=("arbitrary",) * len(grid)
        ),
        cost_estimate=pl.CostEstimate(flops=int(flops), bytes_accessed=int(moved), transcendentals=0),
        input_output_aliases=aliases or {},
        name=name,
    )


def whole(shape):
    zeros = (0,) * len(shape)
    return pl.BlockSpec(shape, lambda i, s: zeros)


def dot_nn(a, b):
    return lax.dot_general(a, b, (((1,), (0,)), ((), ())), preferred_element_type=F32)


def dot_nt(a, b):
    return lax.dot_general(a, b, (((1,), (1,)), ((), ())), preferred_element_type=F32)


def dot_tn(a, b):
    return lax.dot_general(a, b, (((0,), (0,)), ((), ())), preferred_element_type=F32)


def norm_rows(scalars, hidden_rows, norm_gain, chips):
    tokens, width = hidden_rows.shape
    part = width // chips
    tile = 128

    def body(s, x_ref, g_ref, o_ref):
        total = jnp.zeros((tile, 1), F32)
        for b in range(chips):
            x = x_ref[:, b * part : (b + 1) * part].astype(F32)
            total = total + jnp.sum(x * x, axis=-1, keepdims=True)
        factor = lax.rsqrt(total * (1.0 / width) + norm_eps)
        for b in range(chips):
            x = x_ref[:, b * part : (b + 1) * part].astype(F32)
            o_ref[b] = (x * factor * g_ref[:, b * part : (b + 1) * part]).astype(BF16)

    return call(
        body,
        jax.ShapeDtypeStruct((chips, tokens, part), BF16),
        [pl.BlockSpec((tile, width), lambda i, s: (i, 0)), whole((1, width))],
        pl.BlockSpec((chips, tile, part), lambda i, s: (0, i, 0)),
        grid=(tokens // tile,),
        flops=tokens * width * 6,
        moved=tokens * width * 4,
        name="norm",
    )(scalars, hidden_rows, norm_gain.reshape(1, width))


def columns_of(core, head, kv, heads, kv_width):
    return pl.multiple_of(kv * kv_width + (core * heads + head) * HD, HD)


def own_blocks(scalars, weight, received, heads):
    rows, cols = weight.shape

    def body(s, w_ref, r_ref, *o_refs):
        core = s[0]
        mine = pl.multiple_of(core * rows, 16)
        theirs = pl.multiple_of((1 - core) * rows, 16)
        for h in range(heads):
            for kv in range(2):
                there = pl.ds(columns_of(core, h, kv, heads, cols // 2), HD)
                lanes = slice(kv * HD, (kv + 1) * HD)
                o_refs[h][pl.ds(mine, rows), lanes] = w_ref[:, there]
                o_refs[h][pl.ds(theirs, rows), lanes] = r_ref[:, there]

    shape = (2 * rows, 2 * HD)
    return call(
        body,
        [jax.ShapeDtypeStruct(shape, weight.dtype)] * heads,
        [whole((rows, cols))] * 2,
        [whole(shape)] * heads,
        moved=rows * cols * 6,
        name="own_blocks",
    )(scalars, weight, received)


def start_deltas(scalars, blocks, outer, received, heads):
    rows, cols = outer.shape

    def body(s, o_ref, r_ref, *refs):
        core = s[0]
        for h in range(heads):
            block_ref, out_ref = refs[h], refs[heads + h]
            for kv in range(2):
                there = pl.ds(columns_of(core, h, kv, heads, cols // 2), HD)
                mine = o_ref[:, there]
                theirs = r_ref[:, there]
                first = jnp.where(core == 0, mine, theirs)
                second = jnp.where(core == 0, theirs, mine)
                both = jnp.concatenate([first, second], axis=0)
                both = both - block_ref[:, kv * HD : (kv + 1) * HD].astype(F32)
                out_ref[kv * HD : (kv + 1) * HD, :] = both.T

    return call(
        body,
        [jax.ShapeDtypeStruct((2 * HD, 2 * rows), F32)] * heads,
        [whole((rows, cols))] * 2 + [whole((2 * rows, 2 * HD))] * heads,
        [whole((2 * HD, 2 * rows))] * heads,
        moved=rows * cols * 14,
        name="start_deltas",
    )(scalars, outer, received, *blocks)


def group_step(scalars, rows_mine, rows_other, blocks, halves, queries, queries_other, out_grad, out_grad_other, heads):
    chips, tokens, part = rows_mine.shape
    seqs, length, query_width = queries.shape
    own_width = query_width // 2
    repeat = own_width // (heads * HD)
    inv_root = (chips * part) ** (-0.5)
    half = length // 2
    last = chips - 1
    two_power = HD ** (-0.5) * 1.4426950408889634
    wide = 2 * HD

    def body(s, a_ref, b_ref, qa_ref, qb_ref, ga_ref, gb_ref, *refs):
        block_refs = [refs[h * last : (h + 1) * last] for h in range(heads)]
        half_refs = [refs[heads * last + 2 * h : heads * last + 2 * h + 2] for h in range(heads)]
        refs = refs[heads * (last + 2) :]
        sum_refs, up_refs, down_refs = refs[:heads], refs[heads : 2 * heads], refs[2 * heads : 3 * heads]
        held, w_held, q_held, g_held, acc, grads, done = refs[3 * heads : 3 * heads + 7]
        row_sems, w_sems, q_sems, out_sems = refs[3 * heads + 7 :]

        waits = []
        for k in range(chips):
            wait = []
            for side, ref in enumerate((a_ref, b_ref)):
                wait.append(pltpu.make_async_copy(ref.at[s[1 + k]], held.at[k, side], row_sems.at[k, side]))
            for h in range(heads):
                if k < last:
                    wait.append(pltpu.make_async_copy(block_refs[h][k], w_held.at[h, k], w_sems.at[h, k]))
                else:
                    for at in range(2):
                        there = w_held.at[h, k, pl.ds(at * (part // 2), part // 2)]
                        wait.append(pltpu.make_async_copy(half_refs[h][at], there, w_sems.at[h, k + at]))
            waits.append(wait)
        mine = pl.ds(pl.multiple_of(s[0] * own_width, HD), own_width)
        pairs = (
            (qa_ref.at[:, :, mine], q_held.at[pl.ds(0, seqs)]),
            (ga_ref.at[:, :, mine], g_held.at[pl.ds(0, seqs)]),
            (qb_ref.at[:, :, mine], q_held.at[pl.ds(seqs, seqs)]),
            (gb_ref.at[:, :, mine], g_held.at[pl.ds(seqs, seqs)]),
        )
        query_waits = [pltpu.make_async_copy(x, y, q_sems.at[k]) for k, (x, y) in enumerate(pairs)]
        for wait in waits:
            for copy in wait:
                copy.start()
        for copy in query_waits:
            copy.start()

        for k in range(chips):
            for copy in waits[k]:
                copy.wait()
            for h in range(heads):
                for side in range(2):
                    here = slice(side * tokens, (side + 1) * tokens)
                    product = dot_nn(held[k, side], w_held[h, k])
                    acc[h, here, :] = product if k == 0 else acc[h, here, :] + product
        for copy in query_waits:
            copy.wait()

        def one(at, carry):
            token = pl.ds(pl.multiple_of(at * length, length), length)
            for h in range(heads):
                kv = (acc[h, token, :] * inv_root).astype(BF16)
                keys, values = kv[:, :HD], kv[:, HD:]
                found = []
                for t in range(2):
                    upto = (t + 1) * half
                    rows_of = slice(t * half, upto)
                    lanes = [slice((h * repeat + r) * HD, (h * repeat + r + 1) * HD) for r in range(repeat)]
                    q = jnp.concatenate([q_held[at, rows_of, x] for x in lanes], axis=0)
                    g = jnp.concatenate([g_held[at, rows_of, x] for x in lanes], axis=0)
                    scores = dot_nt(keys[:upto], q) * two_power
                    causal = lax.broadcasted_iota(jnp.int32, (half, half), 0) <= lax.broadcasted_iota(
                        jnp.int32, (half, half), 1
                    )
                    causal = jnp.concatenate([causal.astype(F32)] * repeat, axis=1) > 0.0
                    end = jnp.where(causal, scores[upto - half :], -1e30)
                    scores = end if t == 0 else jnp.concatenate([scores[:half], end], axis=0)
                    highest = jnp.max(scores, axis=0, keepdims=True)
                    exps = jnp.exp2(scores - highest)
                    prob = exps * (1.0 / jnp.sum(exps, axis=0, keepdims=True))
                    prob_grad = dot_nt(values[:upto], g).astype(BF16).astype(F32)
                    weighted = prob * prob_grad
                    mean = jnp.sum(weighted, axis=0, keepdims=True)
                    score_grad = (weighted - prob * mean).astype(BF16)
                    found.append((dot_nn(score_grad, q), dot_nn(prob.astype(BF16), g)))
                for kv_at, factor in ((0, HD ** (-0.5)), (1, 1.0)):
                    early, late = found[0][kv_at], found[1][kv_at]
                    grad = jnp.concatenate([(late[:half] + early) * factor, late[half:] * factor], axis=0)
                    grads[h * wide + kv_at * HD : h * wide + (kv_at + 1) * HD, token] = grad.T.astype(BF16)
            return carry

        lax.fori_loop(0, 2 * seqs, one, 0)

        leaving = []
        for k in [last] + list(range(last))[::-1]:
            total = dot_nn(grads[:, :tokens], held[k, 0]) + dot_nn(grads[:, tokens:], held[k, 1])
            total = (total * inv_root).astype(BF16)
            for h in range(heads):
                done[h, k] = total[h * wide : (h + 1) * wide]
                if k < last:
                    leaving.append(pltpu.make_async_copy(done.at[h, k], sum_refs[h].at[k], out_sems.at[h, k]))
                else:
                    for at, ref in enumerate((up_refs[h], down_refs[h])):
                        there = done.at[h, k, pl.ds(at * HD, HD)]
                        leaving.append(pltpu.make_async_copy(there, ref, out_sems.at[h, k + at]))
            for copy in leaving[-heads if k < last else -2 * heads :]:
                copy.start()
        for copy in leaving:
            copy.wait()

    any_spec = pl.BlockSpec(memory_space=pl.ANY)
    inputs = [rows_mine, rows_other, queries, queries_other, out_grad, out_grad_other]
    for h in range(heads):
        inputs += blocks[h]
    for h in range(heads):
        inputs += halves[h]
    flops = 2 * 2 * tokens * chips * part * wide * heads * 2 + heads * 2 * seqs * repeat * length * length * HD * 16
    outs = call(
        body,
        [jax.ShapeDtypeStruct((last, wide, part), BF16)] * heads + [jax.ShapeDtypeStruct((HD, part), BF16)] * (2 * heads),
        [any_spec] * len(inputs),
        [any_spec] * (3 * heads),
        scratch=[
            pltpu.VMEM((chips, 2, tokens, part), BF16),
            pltpu.VMEM((heads, chips, part, wide), BF16),
            pltpu.VMEM((2 * seqs, length, own_width), BF16),
            pltpu.VMEM((2 * seqs, length, own_width), BF16),
            pltpu.VMEM((heads, 2 * tokens, wide), F32),
            pltpu.VMEM((heads * wide, 2 * tokens), BF16),
            pltpu.VMEM((heads, chips, wide, part), BF16),
            pltpu.SemaphoreType.DMA((chips, 2)),
            pltpu.SemaphoreType.DMA((heads, chips + 1)),
            pltpu.SemaphoreType.DMA((4,)),
            pltpu.SemaphoreType.DMA((heads, chips + 1)),
        ],
        flops=flops,
        moved=2 * tokens * chips * part * 6,
        name="group_step",
    )(scalars, *inputs)
    return outs[:heads], outs[heads : 2 * heads], outs[2 * heads :]


def add_partials(scalars, own, up, down, distance, name):
    part = own.shape[-1]
    is_half = up.shape[0] == HD
    at = 2 * distance - 1

    def body(s, ou_ref, od_ref, ui_ref, di_ref, up_ref, down_ref):
        mine_up, mine_down = ou_ref[0].astype(F32), od_ref[0].astype(F32)
        if is_half:
            keys = pl.program_id(0) == 0
            up_ref[...] = jnp.where(keys, mine_up + ui_ref[...].astype(F32), mine_up).astype(BF16)
            down_ref[...] = jnp.where(keys, mine_down, mine_down + di_ref[...].astype(F32)).astype(BF16)
        else:
            up_ref[...] = (mine_up + ui_ref[...].astype(F32)).astype(BF16)
            down_ref[...] = (mine_down + di_ref[...].astype(F32)).astype(BF16)

    block = (HD, part)
    came = whole(block) if is_half else pl.BlockSpec(block, lambda i, s: (i, 0))
    shape = jax.ShapeDtypeStruct((2 * HD, part), BF16)
    return call(
        body,
        [shape] * 2,
        [
            pl.BlockSpec((1, HD, part), lambda i, s: (at, i, 0)),
            pl.BlockSpec((1, HD, part), lambda i, s: (at + 1, i, 0)),
            came,
            came,
        ],
        [pl.BlockSpec(block, lambda i, s: (i, 0))] * 2,
        grid=(2,),
        moved=2 * HD * part * 12,
        name=name,
    )(scalars, own, own, up, down)


def split_packs(values):
    deep = values.shape[0] // 2
    rows = values.shape[1] // 2
    return [
        jnp.concatenate([values[:deep, k * rows : (k + 1) * rows], values[deep:, k * rows : (k + 1) * rows]], axis=1)
        for k in range(2)
    ]


def code_deltas(scalars, own, up, down, delta_start, name):
    part = own.shape[-1]

    def body(s, g_ref, ui_ref, di_ref, d_ref, own_ref, core_ref, y_ref, far_ref):
        core = s[0]
        total = g_ref[0].astype(F32) + ui_ref[...].astype(F32) + di_ref[...].astype(F32)
        delta = d_ref[...] + inner_rate * total
        scales, coded = [], []
        for kv in range(2):
            piece = delta[kv * HD : (kv + 1) * HD]
            scale = (jnp.max(jnp.abs(piece), axis=0, keepdims=True) + scale_eps).astype(BF16).astype(F32)
            scales.append(scale)
            coded.append(piece / scale)
        grads = split_packs(total)
        codes = split_packs(jnp.concatenate(coded, axis=0))
        levels = split_packs(jnp.concatenate(scales, axis=0))
        for mine, wide_ref, thin_ref in ((True, own_ref, y_ref), (False, core_ref, far_ref)):
            first = (core == 0) if mine else (core == 1)
            grad = jnp.where(first, grads[0], grads[1]).astype(BF16)
            code = jnp.where(first, codes[0], codes[1]).astype(BF16)
            level = jnp.where(first, levels[0], levels[1])
            level = jnp.broadcast_to(level, (SCALE_ROWS, part)).astype(BF16)
            wide_ref[:HD, :] = code
            wide_ref[HD : HD + SCALE_ROWS, :] = level
            wide_ref[HD + SCALE_ROWS :, :] = grad
            thin_ref[:HD, :] = code
            thin_ref[HD:, :] = level

    wide, thin = (2 * HD + SCALE_ROWS, part), (HD + SCALE_ROWS, part)
    return call(
        body,
        [jax.ShapeDtypeStruct(shape, BF16) for shape in (wide, wide, thin, thin)],
        [
            pl.BlockSpec((1, 2 * HD, part), lambda i, s: (0, 0, 0)),
            whole(up.shape),
            whole(down.shape),
            whole(delta_start.shape),
        ],
        [whole(wide), whole(wide), whole(thin), whole(thin)],
        moved=2 * HD * part * 16,
        name=name,
    )(scalars, own, up, down, delta_start)


def finish(scalars, weight, outer, momentum, grads, codes, before, head, heads):
    rows, cols = weight.shape
    groups = len(codes[0])
    packs = [*codes[0], grads[0], *codes[1], grads[1]]
    kept = [] if before is None else list(before)
    count = len(packs)

    def body(s, w_ref, k_ref, m_ref, *refs):
        pack_refs = refs[:count]
        out_refs = refs[count + len(kept) : count + len(kept) + 3]
        refs = refs[count + len(kept) + 3 :]
        pack_held = refs[:count]
        w_held, k_held, m_held, blend, stepped, moved, pack_sems, in_sems, out_sems = refs[count:]

        def columns(at):
            core = s[0] if at < 2 else 1 - s[0]
            return pl.ds(columns_of(core, head, at % 2, heads, cols // 2), HD)

        pack_waits = [pltpu.make_async_copy(x, y, pack_sems.at[k]) for k, (x, y) in enumerate(zip(pack_refs, pack_held))]
        waits = []
        for at in range(4):
            held = ((w_ref, w_held), (k_ref, k_held), (m_ref, m_held))
            waits.append([pltpu.make_async_copy(x.at[:, columns(at)], y.at[at], in_sems.at[at, k]) for k, (x, y) in enumerate(held)])
        for copy in pack_waits[: count // 2] + waits[0] + waits[1] + pack_waits[count // 2 :] + waits[2] + waits[3]:
            copy.start()
        leaving = []
        for at in range(4):
            side, kv = at // 2, at % 2
            own = range(side * (groups + 1), (side + 1) * (groups + 1))
            if kv == 0:
                for k in own:
                    pack_waits[k].wait()
            lanes = slice(kv * rows, (kv + 1) * rows)
            grad = pack_held[own[-1]][HD + SCALE_ROWS :, lanes].astype(F32).T
            total = jnp.zeros((HD, rows), F32)
            for k in own[:-1]:
                total = total + pack_held[k][:HD, lanes].astype(F32) * pack_held[k][HD : HD + 1, lanes].astype(F32)
            average = (total / groups).T
            for copy in waits[at]:
                copy.wait()
            fresh = w_held[at].astype(F32) - inner_rate * grad
            moment = momentum_decay * m_held[at] + average
            new = k_held[at] - outer_rate * (momentum_decay * moment + average)
            moved[at] = moment
            stepped[at] = new
            blend[at] = (blend_share * fresh + (1.0 - blend_share) * new).astype(BF16)
            for k, (x, y) in enumerate(zip((blend, stepped, moved), out_refs)):
                leaving.append(pltpu.make_async_copy(x.at[at], y.at[:, columns(at)], out_sems.at[at, k]))
                leaving[-1].start()
        for copy in leaving:
            copy.wait()

    any_spec = pl.BlockSpec(memory_space=pl.ANY)
    return call(
        body,
        [
            jax.ShapeDtypeStruct((rows, cols), BF16),
            jax.ShapeDtypeStruct((rows, cols), F32),
            jax.ShapeDtypeStruct((rows, cols), F32),
        ],
        [any_spec] * (3 + count + len(kept)),
        [any_spec] * 3,
        scratch=[pltpu.VMEM(p.shape, BF16) for p in packs]
        + [pltpu.VMEM((4, rows, HD), t) for t in (BF16, F32, F32, BF16, F32, F32)]
        + [
            pltpu.SemaphoreType.DMA((count,)),
            pltpu.SemaphoreType.DMA((4, 3)),
            pltpu.SemaphoreType.DMA((4, 3)),
        ],
        moved=rows * cols * 12,
        aliases={4 + count + k: k for k in range(len(kept))},
        name=f"finish_{head}",
    )(scalars, weight, outer, momentum, *packs, *kept)


def local(hidden, norm_gain, queries, out_grad, kv_inner, kv_outer, momentum):
    count = lax.axis_size("fsdp")
    groups = lax.axis_size("group")
    index = lax.axis_index("fsdp")
    group = lax.axis_index("group")
    chips = count // 2
    far = chips // 2
    ring = ring_order(chips)
    place = {chip: at for at, chip in enumerate(ring)}
    order = [0] + [k % chips for step in range(1, far) for k in (step, -step)] + [far]
    walks = np.array([[ring[(place[j] + k) % chips] for k in order] for j in range(chips)], np.int32)
    core = index % 2
    scalars = jnp.concatenate([core[None].astype(jnp.int32), jnp.asarray(walks)[index // 2]])

    def around(shift):
        return [(2 * j + c, 2 * ring[(place[j] + shift) % chips] + c) for j in range(chips) for c in range(2)]

    up = functools.partial(lax.ppermute, axis_name="fsdp", perm=around(1))
    down = functools.partial(lax.ppermute, axis_name="fsdp", perm=around(-1))
    swap = functools.partial(lax.ppermute, axis_name="fsdp", perm=[(i, i ^ 1) for i in range(count)])

    def across(values, shift, flip):
        pairs = [
            (g * count + i, (g + shift) % groups * count + (i ^ flip)) for g in range(groups) for i in range(count)
        ]
        return lax.ppermute(values, ("group", "fsdp"), pairs)

    weight = kv_inner[0]
    rows, cols = weight.shape
    heads = cols // 2 // HD // 2
    seqs, length, width = hidden.shape[1:]
    part = 2 * rows

    own = own_blocks(scalars, weight, swap(weight), heads)

    tied = lax.optimization_barrier
    own, outer_other, queries_other = tied((own, swap(kv_outer), swap(queries[0])))
    out_grad_other = swap(tied((out_grad[0], own))[0])
    rows_mine = norm_rows(scalars, tied((hidden, own))[0].reshape(seqs * length, width), norm_gain, chips)

    blocks = [[own[h]] for h in range(heads)]
    halves = [None] * heads
    ups, downs = list(own), list(own)
    for step in range(1, far + 1):
        for h in range(heads):
            if step < far:
                ups[h], downs[h] = up(ups[h]), down(downs[h])
                blocks[h] += [downs[h], ups[h]]
            else:
                halves[h] = (up(ups[h][: part // 2]), down(downs[h][part // 2 :]))
        if step == 1:
            rows_other = swap(tied((rows_mine, out_grad_other, ups, downs))[0])
    deltas = start_deltas(scalars, own, kv_outer, outer_other, heads)

    rows_mine, deltas = lax.optimization_barrier((rows_mine, deltas))
    sums, far_up, far_down = group_step(
        scalars, rows_mine, rows_other, blocks, halves, queries[0], queries_other, out_grad[0], out_grad_other, heads
    )

    outs = None
    for h in range(heads):
        going_up, going_down = far_up[h], far_down[h]
        for distance in range(far - 1, 0, -1):
            going_up, going_down = add_partials(
                scalars, sums[h], up(going_up), down(going_down), distance, f"add_{h}_{distance}"
            )
        own_pack, core_pack, thin_own, thin_core = code_deltas(
            scalars, sums[h], up(going_up), down(going_down), deltas[h], f"code_{h}"
        )
        from_core = swap(core_pack)
        mine = [own_pack] + [across(thin_own, k, 0) for k in range(1, groups)]
        theirs = [from_core] + [across(thin_core, k, 1) for k in range(1, groups)]
        if groups > 2:
            deep = HD + SCALE_ROWS
            ordered = []
            for packs in (mine, theirs):
                stacked = jnp.stack([p[:deep] for p in packs])
                ordered.append([stacked[(group - g) % groups] for g in range(groups)])
            mine, theirs = ordered
        outs = finish(
            scalars, weight, kv_outer, momentum, (own_pack, from_core), (mine, theirs), outs, h, heads
        )

    blended, outer_new, momentum_new = outs
    return (blended[None], outer_new, momentum_new)


def solution(mesh):
    in_specs = (
        P("group", "fsdp", None, None),
        P(),
        P("group", "fsdp", None, None),
        P("group", "fsdp", None, None),
        P("group", "fsdp", None),
        P("fsdp", None),
        P("fsdp", None),
    )
    out_specs = (P("group", "fsdp", None), P("fsdp", None), P("fsdp", None))
    return jax.shard_map(local, mesh=mesh, in_specs=in_specs, out_specs=out_specs, check_vma=False)
```

```python
import functools

import jax
import jax.numpy as jnp
import numpy as np
from jax import lax
from jax.experimental import pallas as pl
from jax.experimental.pallas import tpu as pltpu
from jax.sharding import PartitionSpec as P

HD = 128

inner_rate = 0.25
outer_rate = 0.7
momentum_decay = 0.9
blend_share = 0.5
norm_eps = 1e-06
scale_eps = 1e-06

F32 = jnp.float32
BF16 = jnp.bfloat16
VMEM_LIMIT = 64 * 1024 * 1024 - 65536
SCALE_ROWS = 16


def ring_order(count):
    return list(range(0, count, 2)) + list(range(1, count, 2))[::-1]


def call(body, out_shape, in_specs, out_specs, grid=(1,), scratch=(), flops=0, moved=0, aliases=None, name=None):
    return pl.pallas_call(
        body,
        out_shape=out_shape,
        grid_spec=pltpu.PrefetchScalarGridSpec(
            num_scalar_prefetch=1,
            grid=grid,
            in_specs=in_specs,
            out_specs=out_specs,
            scratch_shapes=list(scratch),
        ),
        compiler_params=pltpu.CompilerParams(
            vmem_limit_bytes=VMEM_LIMIT, dimension_semantics=("arbitrary",) * len(grid)
        ),
        cost_estimate=pl.CostEstimate(flops=int(flops), bytes_accessed=int(moved), transcendentals=0),
        input_output_aliases=aliases or {},
        name=name,
    )


def whole(shape):
    zeros = (0,) * len(shape)
    return pl.BlockSpec(shape, lambda i, s: zeros)


def dot_nn(a, b):
    return lax.dot_general(a, b, (((1,), (0,)), ((), ())), preferred_element_type=F32)


def dot_nt(a, b):
    return lax.dot_general(a, b, (((1,), (1,)), ((), ())), preferred_element_type=F32)


def dot_tn(a, b):
    return lax.dot_general(a, b, (((0,), (0,)), ((), ())), preferred_element_type=F32)


def norm_rows(scalars, hidden_rows, norm_gain, chips):
    tokens, width = hidden_rows.shape
    part = width // chips
    tile = 128

    def body(s, x_ref, g_ref, o_ref):
        total = jnp.zeros((tile, 1), F32)
        for b in range(chips):
            x = x_ref[:, b * part : (b + 1) * part].astype(F32)
            total = total + jnp.sum(x * x, axis=-1, keepdims=True)
        factor = lax.rsqrt(total * (1.0 / width) + norm_eps)
        for b in range(chips):
            x = x_ref[:, b * part : (b + 1) * part].astype(F32)
            o_ref[b] = (x * factor * g_ref[:, b * part : (b + 1) * part]).astype(BF16)

    return call(
        body,
        jax.ShapeDtypeStruct((chips, tokens, part), BF16),
        [pl.BlockSpec((tile, width), lambda i, s: (i, 0)), whole((1, width))],
        pl.BlockSpec((chips, tile, part), lambda i, s: (0, i, 0)),
        grid=(tokens // tile,),
        flops=tokens * width * 6,
        moved=tokens * width * 4,
        name="norm",
    )(scalars, hidden_rows, norm_gain.reshape(1, width))


def columns_of(core, head, kv, heads, kv_width):
    return pl.multiple_of(kv * kv_width + (core * heads + head) * HD, HD)


def own_blocks(scalars, weight, received, heads):
    rows, cols = weight.shape

    def body(s, w_ref, r_ref, *o_refs):
        core = s[0]
        mine = pl.multiple_of(core * rows, 16)
        theirs = pl.multiple_of((1 - core) * rows, 16)
        for h in range(heads):
            for kv in range(2):
                there = pl.ds(columns_of(core, h, kv, heads, cols // 2), HD)
                lanes = slice(kv * HD, (kv + 1) * HD)
                o_refs[h][pl.ds(mine, rows), lanes] = w_ref[:, there]
                o_refs[h][pl.ds(theirs, rows), lanes] = r_ref[:, there]

    shape = (2 * rows, 2 * HD)
    return call(
        body,
        [jax.ShapeDtypeStruct(shape, weight.dtype)] * heads,
        [whole((rows, cols))] * 2,
        [whole(shape)] * heads,
        moved=rows * cols * 6,
        name="own_blocks",
    )(scalars, weight, received)


def start_deltas(scalars, blocks, outer, received, heads):
    rows, cols = outer.shape

    def body(s, o_ref, r_ref, *refs):
        core = s[0]
        for h in range(heads):
            block_ref, out_ref = refs[h], refs[heads + h]
            for kv in range(2):
                there = pl.ds(columns_of(core, h, kv, heads, cols // 2), HD)
                mine = o_ref[:, there]
                theirs = r_ref[:, there]
                first = jnp.where(core == 0, mine, theirs)
                second = jnp.where(core == 0, theirs, mine)
                both = jnp.concatenate([first, second], axis=0)
                both = both - block_ref[:, kv * HD : (kv + 1) * HD].astype(F32)
                out_ref[kv * HD : (kv + 1) * HD, :] = both.T

    return call(
        body,
        [jax.ShapeDtypeStruct((2 * HD, 2 * rows), F32)] * heads,
        [whole((rows, cols))] * 2 + [whole((2 * rows, 2 * HD))] * heads,
        [whole((2 * HD, 2 * rows))] * heads,
        moved=rows * cols * 14,
        name="start_deltas",
    )(scalars, outer, received, *blocks)


def group_step(scalars, rows_mine, rows_other, blocks, halves, queries, queries_other, out_grad, out_grad_other, heads):
    chips, tokens, part = rows_mine.shape
    seqs, length, query_width = queries.shape
    own_width = query_width // 2
    repeat = own_width // (heads * HD)
    inv_root = (chips * part) ** (-0.5)
    half = length // 2
    last = chips - 1
    two_power = HD ** (-0.5) * 1.4426950408889634
    wide = 2 * HD

    def body(s, a_ref, b_ref, qa_ref, qb_ref, ga_ref, gb_ref, *refs):
        block_refs = [refs[h * last : (h + 1) * last] for h in range(heads)]
        half_refs = [refs[heads * last + 2 * h : heads * last + 2 * h + 2] for h in range(heads)]
        refs = refs[heads * (last + 2) :]
        sum_refs, up_refs, down_refs = refs[:heads], refs[heads : 2 * heads], refs[2 * heads : 3 * heads]
        held, w_held, q_held, g_held, acc, grads, done = refs[3 * heads : 3 * heads + 7]
        row_sems, w_sems, q_sems, out_sems = refs[3 * heads + 7 :]

        waits = []
        for k in range(chips):
            wait = []
            for side, ref in enumerate((a_ref, b_ref)):
                wait.append(pltpu.make_async_copy(ref.at[s[1 + k]], held.at[k, side], row_sems.at[k, side]))
            for h in range(heads):
                if k < last:
                    wait.append(pltpu.make_async_copy(block_refs[h][k], w_held.at[h, k], w_sems.at[h, k]))
                else:
                    for at in range(2):
                        there = w_held.at[h, k, pl.ds(at * (part // 2), part // 2)]
                        wait.append(pltpu.make_async_copy(half_refs[h][at], there, w_sems.at[h, k + at]))
            waits.append(wait)
        mine = pl.ds(pl.multiple_of(s[0] * own_width, HD), own_width)
        pairs = (
            (qa_ref.at[:, :, mine], q_held.at[pl.ds(0, seqs)]),
            (ga_ref.at[:, :, mine], g_held.at[pl.ds(0, seqs)]),
            (qb_ref.at[:, :, mine], q_held.at[pl.ds(seqs, seqs)]),
            (gb_ref.at[:, :, mine], g_held.at[pl.ds(seqs, seqs)]),
        )
        query_waits = [pltpu.make_async_copy(x, y, q_sems.at[k]) for k, (x, y) in enumerate(pairs)]
        ahead = 3
        waits.append(query_waits)
        for k in range(ahead):
            for copy in waits[k]:
                copy.start()

        for k in range(chips):
            if k + ahead <= chips:
                for copy in waits[k + ahead]:
                    copy.start()
            for copy in waits[k]:
                copy.wait()
            for h in range(heads):
                for side in range(2):
                    here = slice(side * tokens, (side + 1) * tokens)
                    product = dot_nn(held[k, side], w_held[h, k])
                    acc[h, here, :] = product if k == 0 else acc[h, here, :] + product
        for copy in query_waits:
            copy.wait()

        def one(at, carry):
            token = pl.ds(pl.multiple_of(at * length, length), length)
            for h in range(heads):
                kv = (acc[h, token, :] * inv_root).astype(BF16)
                keys, values = kv[:, :HD], kv[:, HD:]
                found = []
                for t in range(2):
                    upto = (t + 1) * half
                    rows_of = slice(t * half, upto)
                    lanes = [slice((h * repeat + r) * HD, (h * repeat + r + 1) * HD) for r in range(repeat)]
                    q = jnp.concatenate([q_held[at, rows_of, x] for x in lanes], axis=0)
                    g = jnp.concatenate([g_held[at, rows_of, x] for x in lanes], axis=0)
                    scores = dot_nt(keys[:upto], q) * two_power
                    causal = lax.broadcasted_iota(jnp.int32, (half, half), 0) <= lax.broadcasted_iota(
                        jnp.int32, (half, half), 1
                    )
                    causal = jnp.concatenate([causal.astype(F32)] * repeat, axis=1) > 0.0
                    end = jnp.where(causal, scores[upto - half :], -1e30)
                    scores = end if t == 0 else jnp.concatenate([scores[:half], end], axis=0)
                    highest = jnp.max(scores, axis=0, keepdims=True)
                    exps = jnp.exp2(scores - highest)
                    prob = exps * (1.0 / jnp.sum(exps, axis=0, keepdims=True))
                    prob_grad = dot_nt(values[:upto], g).astype(BF16).astype(F32)
                    weighted = prob * prob_grad
                    mean = jnp.sum(weighted, axis=0, keepdims=True)
                    score_grad = (weighted - prob * mean).astype(BF16)
                    found.append((dot_nn(score_grad, q), dot_nn(prob.astype(BF16), g)))
                for kv_at, factor in ((0, HD ** (-0.5)), (1, 1.0)):
                    early, late = found[0][kv_at], found[1][kv_at]
                    grad = jnp.concatenate([(late[:half] + early) * factor, late[half:] * factor], axis=0)
                    grads[h * wide + kv_at * HD : h * wide + (kv_at + 1) * HD, token] = grad.T.astype(BF16)
            return carry

        lax.fori_loop(0, 2 * seqs, one, 0)

        leaving = []
        for k in [last] + list(range(last))[::-1]:
            total = dot_nn(grads[:, :tokens], held[k, 0]) + dot_nn(grads[:, tokens:], held[k, 1])
            total = (total * inv_root).astype(BF16)
            for h in range(heads):
                done[h, k] = total[h * wide : (h + 1) * wide]
                if k < last:
                    leaving.append(pltpu.make_async_copy(done.at[h, k], sum_refs[h].at[k], out_sems.at[h, k]))
                else:
                    for at, ref in enumerate((up_refs[h], down_refs[h])):
                        there = done.at[h, k, pl.ds(at * HD, HD)]
                        leaving.append(pltpu.make_async_copy(there, ref, out_sems.at[h, k + at]))
            for copy in leaving[-heads if k < last else -2 * heads :]:
                copy.start()
        for copy in leaving:
            copy.wait()

    any_spec = pl.BlockSpec(memory_space=pl.ANY)
    inputs = [rows_mine, rows_other, queries, queries_other, out_grad, out_grad_other]
    for h in range(heads):
        inputs += blocks[h]
    for h in range(heads):
        inputs += halves[h]
    flops = 2 * 2 * tokens * chips * part * wide * heads * 2 + heads * 2 * seqs * repeat * length * length * HD * 16
    outs = call(
        body,
        [jax.ShapeDtypeStruct((last, wide, part), BF16)] * heads + [jax.ShapeDtypeStruct((HD, part), BF16)] * (2 * heads),
        [any_spec] * len(inputs),
        [any_spec] * (3 * heads),
        scratch=[
            pltpu.VMEM((chips, 2, tokens, part), BF16),
            pltpu.VMEM((heads, chips, part, wide), BF16),
            pltpu.VMEM((2 * seqs, length, own_width), BF16),
            pltpu.VMEM((2 * seqs, length, own_width), BF16),
            pltpu.VMEM((heads, 2 * tokens, wide), F32),
            pltpu.VMEM((heads * wide, 2 * tokens), BF16),
            pltpu.VMEM((heads, chips, wide, part), BF16),
            pltpu.SemaphoreType.DMA((chips, 2)),
            pltpu.SemaphoreType.DMA((heads, chips + 1)),
            pltpu.SemaphoreType.DMA((4,)),
            pltpu.SemaphoreType.DMA((heads, chips + 1)),
        ],
        flops=flops,
        moved=2 * tokens * chips * part * 6,
        name="group_step",
    )(scalars, *inputs)
    return outs[:heads], outs[heads : 2 * heads], outs[2 * heads :]


def add_partials(scalars, own, up, down, distance, name):
    part = own.shape[-1]
    is_half = up.shape[0] == HD
    at = 2 * distance - 1

    def body(s, ou_ref, od_ref, ui_ref, di_ref, up_ref, down_ref):
        mine_up, mine_down = ou_ref[0].astype(F32), od_ref[0].astype(F32)
        if is_half:
            keys = pl.program_id(0) == 0
            up_ref[...] = jnp.where(keys, mine_up + ui_ref[...].astype(F32), mine_up).astype(BF16)
            down_ref[...] = jnp.where(keys, mine_down, mine_down + di_ref[...].astype(F32)).astype(BF16)
        else:
            up_ref[...] = (mine_up + ui_ref[...].astype(F32)).astype(BF16)
            down_ref[...] = (mine_down + di_ref[...].astype(F32)).astype(BF16)

    block = (HD, part)
    came = whole(block) if is_half else pl.BlockSpec(block, lambda i, s: (i, 0))
    shape = jax.ShapeDtypeStruct((2 * HD, part), BF16)
    return call(
        body,
        [shape] * 2,
        [
            pl.BlockSpec((1, HD, part), lambda i, s: (at, i, 0)),
            pl.BlockSpec((1, HD, part), lambda i, s: (at + 1, i, 0)),
            came,
            came,
        ],
        [pl.BlockSpec(block, lambda i, s: (i, 0))] * 2,
        grid=(2,),
        moved=2 * HD * part * 12,
        name=name,
    )(scalars, own, own, up, down)


def split_packs(values):
    deep = values.shape[0] // 2
    rows = values.shape[1] // 2
    return [
        jnp.concatenate([values[:deep, k * rows : (k + 1) * rows], values[deep:, k * rows : (k + 1) * rows]], axis=1)
        for k in range(2)
    ]


def code_deltas(scalars, own, up, down, delta_start, name):
    part = own.shape[-1]

    def body(s, g_ref, ui_ref, di_ref, d_ref, own_ref, core_ref, y_ref, far_ref):
        core = s[0]
        total = g_ref[0].astype(F32) + ui_ref[...].astype(F32) + di_ref[...].astype(F32)
        delta = d_ref[...] + inner_rate * total
        scales, coded = [], []
        for kv in range(2):
            piece = delta[kv * HD : (kv + 1) * HD]
            scale = (jnp.max(jnp.abs(piece), axis=0, keepdims=True) + scale_eps).astype(BF16).astype(F32)
            scales.append(scale)
            coded.append(piece / scale)
        grads = split_packs(total)
        codes = split_packs(jnp.concatenate(coded, axis=0))
        levels = split_packs(jnp.concatenate(scales, axis=0))
        for mine, wide_ref, thin_ref in ((True, own_ref, y_ref), (False, core_ref, far_ref)):
            first = (core == 0) if mine else (core == 1)
            grad = jnp.where(first, grads[0], grads[1]).astype(BF16)
            code = jnp.where(first, codes[0], codes[1]).astype(BF16)
            level = jnp.where(first, levels[0], levels[1])
            level = jnp.broadcast_to(level, (SCALE_ROWS, part)).astype(BF16)
            wide_ref[:HD, :] = code
            wide_ref[HD : HD + SCALE_ROWS, :] = level
            wide_ref[HD + SCALE_ROWS :, :] = grad
            thin_ref[:HD, :] = code
            thin_ref[HD:, :] = level

    wide, thin = (2 * HD + SCALE_ROWS, part), (HD + SCALE_ROWS, part)
    return call(
        body,
        [jax.ShapeDtypeStruct(shape, BF16) for shape in (wide, wide, thin, thin)],
        [
            pl.BlockSpec((1, 2 * HD, part), lambda i, s: (0, 0, 0)),
            whole(up.shape),
            whole(down.shape),
            whole(delta_start.shape),
        ],
        [whole(wide), whole(wide), whole(thin), whole(thin)],
        moved=2 * HD * part * 16,
        name=name,
    )(scalars, own, up, down, delta_start)


def finish(scalars, weight, outer, momentum, grads, codes, before, head, heads):
    rows, cols = weight.shape
    groups = len(codes[0])
    packs = [*codes[0], grads[0], *codes[1], grads[1]]
    kept = [] if before is None else list(before)
    count = len(packs)

    def body(s, w_ref, k_ref, m_ref, *refs):
        pack_refs = refs[:count]
        out_refs = refs[count + len(kept) : count + len(kept) + 3]
        refs = refs[count + len(kept) + 3 :]
        pack_held = refs[:count]
        w_held, k_held, m_held, blend, stepped, moved, pack_sems, in_sems, out_sems = refs[count:]

        def columns(at):
            core = s[0] if at < 2 else 1 - s[0]
            return pl.ds(columns_of(core, head, at % 2, heads, cols // 2), HD)

        pack_waits = [pltpu.make_async_copy(x, y, pack_sems.at[k]) for k, (x, y) in enumerate(zip(pack_refs, pack_held))]
        waits = []
        for at in range(4):
            held = ((w_ref, w_held), (k_ref, k_held), (m_ref, m_held))
            waits.append([pltpu.make_async_copy(x.at[:, columns(at)], y.at[at], in_sems.at[at, k]) for k, (x, y) in enumerate(held)])
        for copy in pack_waits[: count // 2] + waits[0] + waits[1] + pack_waits[count // 2 :] + waits[2] + waits[3]:
            copy.start()
        leaving = []
        for at in range(4):
            side, kv = at // 2, at % 2
            own = range(side * (groups + 1), (side + 1) * (groups + 1))
            if kv == 0:
                for k in own:
                    pack_waits[k].wait()
            lanes = slice(kv * rows, (kv + 1) * rows)
            grad = pack_held[own[-1]][HD + SCALE_ROWS :, lanes].astype(F32).T
            total = jnp.zeros((HD, rows), F32)
            for k in own[:-1]:
                total = total + pack_held[k][:HD, lanes].astype(F32) * pack_held[k][HD : HD + 1, lanes].astype(F32)
            average = (total / groups).T
            for copy in waits[at]:
                copy.wait()
            fresh = w_held[at].astype(F32) - inner_rate * grad
            moment = momentum_decay * m_held[at] + average
            new = k_held[at] - outer_rate * (momentum_decay * moment + average)
            moved[at] = moment
            stepped[at] = new
            blend[at] = (blend_share * fresh + (1.0 - blend_share) * new).astype(BF16)
            for k, (x, y) in enumerate(zip((blend, stepped, moved), out_refs)):
                leaving.append(pltpu.make_async_copy(x.at[at], y.at[:, columns(at)], out_sems.at[at, k]))
                leaving[-1].start()
        for copy in leaving:
            copy.wait()

    any_spec = pl.BlockSpec(memory_space=pl.ANY)
    return call(
        body,
        [
            jax.ShapeDtypeStruct((rows, cols), BF16),
            jax.ShapeDtypeStruct((rows, cols), F32),
            jax.ShapeDtypeStruct((rows, cols), F32),
        ],
        [any_spec] * (3 + count + len(kept)),
        [any_spec] * 3,
        scratch=[pltpu.VMEM(p.shape, BF16) for p in packs]
        + [pltpu.VMEM((4, rows, HD), t) for t in (BF16, F32, F32, BF16, F32, F32)]
        + [
            pltpu.SemaphoreType.DMA((count,)),
            pltpu.SemaphoreType.DMA((4, 3)),
            pltpu.SemaphoreType.DMA((4, 3)),
        ],
        moved=rows * cols * 12,
        aliases={4 + count + k: k for k in range(len(kept))},
        name=f"finish_{head}",
    )(scalars, weight, outer, momentum, *packs, *kept)


def local(hidden, norm_gain, queries, out_grad, kv_inner, kv_outer, momentum):
    count = lax.axis_size("fsdp")
    groups = lax.axis_size("group")
    index = lax.axis_index("fsdp")
    group = lax.axis_index("group")
    chips = count // 2
    far = chips // 2
    ring = ring_order(chips)
    place = {chip: at for at, chip in enumerate(ring)}
    order = [0] + [k % chips for step in range(1, far) for k in (step, -step)] + [far]
    walks = np.array([[ring[(place[j] + k) % chips] for k in order] for j in range(chips)], np.int32)
    core = index % 2
    scalars = jnp.concatenate([core[None].astype(jnp.int32), jnp.asarray(walks)[index // 2]])

    def around(shift):
        return [(2 * j + c, 2 * ring[(place[j] + shift) % chips] + c) for j in range(chips) for c in range(2)]

    up = functools.partial(lax.ppermute, axis_name="fsdp", perm=around(1))
    down = functools.partial(lax.ppermute, axis_name="fsdp", perm=around(-1))
    swap = functools.partial(lax.ppermute, axis_name="fsdp", perm=[(i, i ^ 1) for i in range(count)])

    def across(values, shift, flip):
        pairs = [
            (g * count + i, (g + shift) % groups * count + (i ^ flip)) for g in range(groups) for i in range(count)
        ]
        return lax.ppermute(values, ("group", "fsdp"), pairs)

    weight = kv_inner[0]
    rows, cols = weight.shape
    heads = cols // 2 // HD // 2
    seqs, length, width = hidden.shape[1:]
    part = 2 * rows

    received = swap(weight)
    own = own_blocks(scalars, weight, received, heads)

    tied = lax.optimization_barrier
    own, outer_other = tied((own, swap(kv_outer)))
    queries_other = swap(tied((queries[0], received))[0])
    out_grad_other = swap(tied((out_grad[0], own))[0])
    rows_mine = norm_rows(scalars, tied((hidden, own))[0].reshape(seqs * length, width), norm_gain, chips)

    blocks = [[own[h]] for h in range(heads)]
    halves = [None] * heads
    ups, downs = list(own), list(own)
    for step in range(1, far + 1):
        for h in range(heads):
            if step < far:
                ups[h], downs[h] = up(ups[h]), down(downs[h])
                blocks[h] += [downs[h], ups[h]]
            else:
                halves[h] = (up(ups[h][: part // 2]), down(downs[h][part // 2 :]))
        if step == 1:
            rows_other = swap(tied((rows_mine, queries_other, out_grad_other, ups, downs))[0])
    deltas = start_deltas(scalars, own, kv_outer, outer_other, heads)

    rows_mine, deltas = lax.optimization_barrier((rows_mine, deltas))
    sums, far_up, far_down = group_step(
        scalars, rows_mine, rows_other, blocks, halves, queries[0], queries_other, out_grad[0], out_grad_other, heads
    )

    outs = None
    for h in range(heads):
        going_up, going_down = far_up[h], far_down[h]
        for distance in range(far - 1, 0, -1):
            going_up, going_down = add_partials(
                scalars, sums[h], up(going_up), down(going_down), distance, f"add_{h}_{distance}"
            )
        own_pack, core_pack, thin_own, thin_core = code_deltas(
            scalars, sums[h], up(going_up), down(going_down), deltas[h], f"code_{h}"
        )
        from_core = swap(core_pack)
        mine = [own_pack] + [across(thin_own, k, 0) for k in range(1, groups)]
        theirs = [from_core] + [across(thin_core, k, 1) for k in range(1, groups)]
        if groups > 2:
            deep = HD + SCALE_ROWS
            ordered = []
            for packs in (mine, theirs):
                stacked = jnp.stack([p[:deep] for p in packs])
                ordered.append([stacked[(group - g) % groups] for g in range(groups)])
            mine, theirs = ordered
        outs = finish(
            scalars, weight, kv_outer, momentum, (own_pack, from_core), (mine, theirs), outs, h, heads
        )

    blended, outer_new, momentum_new = outs
    return (blended[None], outer_new, momentum_new)


def solution(mesh):
    in_specs = (
        P("group", "fsdp", None, None),
        P(),
        P("group", "fsdp", None, None),
        P("group", "fsdp", None, None),
        P("group", "fsdp", None),
        P("fsdp", None),
        P("fsdp", None),
    )
    out_specs = (P("group", "fsdp", None), P("fsdp", None), P("fsdp", None))
    return jax.shard_map(local, mesh=mesh, in_specs=in_specs, out_specs=out_specs, check_vma=False)
```

```python
import functools

import jax
import jax.numpy as jnp
import numpy as np
from jax import lax
from jax.experimental import pallas as pl
from jax.experimental.pallas import tpu as pltpu
from jax.sharding import PartitionSpec as P

HD = 128

inner_rate = 0.25
outer_rate = 0.7
momentum_decay = 0.9
blend_share = 0.5
norm_eps = 1e-06
scale_eps = 1e-06

F32 = jnp.float32
BF16 = jnp.bfloat16
VMEM_LIMIT = 64 * 1024 * 1024 - 65536
SCALE_ROWS = 16


def ring_order(count):
    return list(range(0, count, 2)) + list(range(1, count, 2))[::-1]


def call(body, out_shape, in_specs, out_specs, grid=(1,), scratch=(), flops=0, moved=0, aliases=None, name=None):
    return pl.pallas_call(
        body,
        out_shape=out_shape,
        grid_spec=pltpu.PrefetchScalarGridSpec(
            num_scalar_prefetch=1,
            grid=grid,
            in_specs=in_specs,
            out_specs=out_specs,
            scratch_shapes=list(scratch),
        ),
        compiler_params=pltpu.CompilerParams(
            vmem_limit_bytes=VMEM_LIMIT, dimension_semantics=("arbitrary",) * len(grid)
        ),
        cost_estimate=pl.CostEstimate(flops=int(flops), bytes_accessed=int(moved), transcendentals=0),
        input_output_aliases=aliases or {},
        name=name,
    )


def whole(shape):
    zeros = (0,) * len(shape)
    return pl.BlockSpec(shape, lambda i, s: zeros)


def dot_nn(a, b):
    return lax.dot_general(a, b, (((1,), (0,)), ((), ())), preferred_element_type=F32)


def dot_nt(a, b):
    return lax.dot_general(a, b, (((1,), (1,)), ((), ())), preferred_element_type=F32)


def dot_tn(a, b):
    return lax.dot_general(a, b, (((0,), (0,)), ((), ())), preferred_element_type=F32)


def norm_rows(scalars, hidden_rows, norm_gain, chips):
    tokens, width = hidden_rows.shape
    part = width // chips
    tile = 128

    def body(s, x_ref, g_ref, o_ref):
        total = jnp.zeros((tile, 1), F32)
        for b in range(chips):
            x = x_ref[:, b * part : (b + 1) * part].astype(F32)
            total = total + jnp.sum(x * x, axis=-1, keepdims=True)
        factor = lax.rsqrt(total * (1.0 / width) + norm_eps)
        for b in range(chips):
            x = x_ref[:, b * part : (b + 1) * part].astype(F32)
            o_ref[b] = (x * factor * g_ref[:, b * part : (b + 1) * part]).astype(BF16)

    return call(
        body,
        jax.ShapeDtypeStruct((chips, tokens, part), BF16),
        [pl.BlockSpec((tile, width), lambda i, s: (i, 0)), whole((1, width))],
        pl.BlockSpec((chips, tile, part), lambda i, s: (0, i, 0)),
        grid=(tokens // tile,),
        flops=tokens * width * 6,
        moved=tokens * width * 4,
        name="norm",
    )(scalars, hidden_rows, norm_gain.reshape(1, width))


def columns_of(core, head, kv, heads, kv_width):
    return pl.multiple_of(kv * kv_width + (core * heads + head) * HD, HD)


def own_blocks(scalars, weight, received, heads):
    rows, cols = weight.shape

    def body(s, w_ref, r_ref, *o_refs):
        core = s[0]
        mine = pl.multiple_of(core * rows, 16)
        theirs = pl.multiple_of((1 - core) * rows, 16)
        for h in range(heads):
            for kv in range(2):
                there = pl.ds(columns_of(core, h, kv, heads, cols // 2), HD)
                lanes = slice(kv * HD, (kv + 1) * HD)
                o_refs[h][pl.ds(mine, rows), lanes] = w_ref[:, there]
                o_refs[h][pl.ds(theirs, rows), lanes] = r_ref[:, there]

    shape = (2 * rows, 2 * HD)
    return call(
        body,
        [jax.ShapeDtypeStruct(shape, weight.dtype)] * heads,
        [whole((rows, cols))] * 2,
        [whole(shape)] * heads,
        moved=rows * cols * 6,
        name="own_blocks",
    )(scalars, weight, received)


def start_deltas(scalars, blocks, outer, received, heads):
    rows, cols = outer.shape

    def body(s, o_ref, r_ref, *refs):
        core = s[0]
        for h in range(heads):
            block_ref, out_ref = refs[h], refs[heads + h]
            for kv in range(2):
                there = pl.ds(columns_of(core, h, kv, heads, cols // 2), HD)
                mine = o_ref[:, there]
                theirs = r_ref[:, there]
                first = jnp.where(core == 0, mine, theirs)
                second = jnp.where(core == 0, theirs, mine)
                both = jnp.concatenate([first, second], axis=0)
                both = both - block_ref[:, kv * HD : (kv + 1) * HD].astype(F32)
                out_ref[kv * HD : (kv + 1) * HD, :] = both.T

    return call(
        body,
        [jax.ShapeDtypeStruct((2 * HD, 2 * rows), F32)] * heads,
        [whole((rows, cols))] * 2 + [whole((2 * rows, 2 * HD))] * heads,
        [whole((2 * HD, 2 * rows))] * heads,
        moved=rows * cols * 14,
        name="start_deltas",
    )(scalars, outer, received, *blocks)


def group_step(scalars, rows_mine, rows_other, blocks, queries, queries_other, out_grad, out_grad_other, heads):
    chips, tokens, part = rows_mine.shape
    seqs, length, query_width = queries.shape
    own_width = query_width // 2
    repeat = own_width // (heads * HD)
    inv_root = (chips * part) ** (-0.5)
    half = length // 2
    last = chips - 1
    two_power = HD ** (-0.5) * 1.4426950408889634
    wide = 2 * HD

    def body(s, a_ref, b_ref, qa_ref, qb_ref, ga_ref, gb_ref, *refs):
        block_refs = [refs[h * chips : (h + 1) * chips] for h in range(heads)]
        refs = refs[heads * chips :]
        sum_refs, up_refs, down_refs = refs[:heads], refs[heads : 2 * heads], refs[2 * heads : 3 * heads]
        held, w_held, q_held, g_held, acc, grads, done = refs[3 * heads : 3 * heads + 7]
        row_sems, w_sems, q_sems, out_sems = refs[3 * heads + 7 :]

        waits = []
        for k in range(chips):
            wait = []
            for side, ref in enumerate((a_ref, b_ref)):
                wait.append(pltpu.make_async_copy(ref.at[s[1 + k]], held.at[k, side], row_sems.at[k, side]))
            for h in range(heads):
                wait.append(pltpu.make_async_copy(block_refs[h][k], w_held.at[h, k], w_sems.at[h, k]))
            waits.append(wait)
        mine = pl.ds(pl.multiple_of(s[0] * own_width, HD), own_width)
        pairs = (
            (qa_ref.at[:, :, mine], q_held.at[pl.ds(0, seqs)]),
            (ga_ref.at[:, :, mine], g_held.at[pl.ds(0, seqs)]),
            (qb_ref.at[:, :, mine], q_held.at[pl.ds(seqs, seqs)]),
            (gb_ref.at[:, :, mine], g_held.at[pl.ds(seqs, seqs)]),
        )
        query_waits = [pltpu.make_async_copy(x, y, q_sems.at[k]) for k, (x, y) in enumerate(pairs)]
        ahead = 3
        waits.append(query_waits)
        for k in range(ahead):
            for copy in waits[k]:
                copy.start()

        for k in range(chips):
            if k + ahead <= chips:
                for copy in waits[k + ahead]:
                    copy.start()
            for copy in waits[k]:
                copy.wait()
            for h in range(heads):
                for side in range(2):
                    here = slice(side * tokens, (side + 1) * tokens)
                    product = dot_nn(held[k, side], w_held[h, k])
                    acc[h, here, :] = product if k == 0 else acc[h, here, :] + product
        for copy in query_waits:
            copy.wait()

        def one(at, carry):
            token = pl.ds(pl.multiple_of(at * length, length), length)
            for h in range(heads):
                kv = (acc[h, token, :] * inv_root).astype(BF16)
                keys, values = kv[:, :HD], kv[:, HD:]
                found = []
                for t in range(2):
                    upto = (t + 1) * half
                    rows_of = slice(t * half, upto)
                    lanes = [slice((h * repeat + r) * HD, (h * repeat + r + 1) * HD) for r in range(repeat)]
                    q = jnp.concatenate([q_held[at, rows_of, x] for x in lanes], axis=0)
                    g = jnp.concatenate([g_held[at, rows_of, x] for x in lanes], axis=0)
                    scores = dot_nt(keys[:upto], q) * two_power
                    causal = lax.broadcasted_iota(jnp.int32, (half, half), 0) <= lax.broadcasted_iota(
                        jnp.int32, (half, half), 1
                    )
                    causal = jnp.concatenate([causal.astype(F32)] * repeat, axis=1) > 0.0
                    end = jnp.where(causal, scores[upto - half :], -1e30)
                    scores = end if t == 0 else jnp.concatenate([scores[:half], end], axis=0)
                    highest = jnp.max(scores, axis=0, keepdims=True)
                    exps = jnp.exp2(scores - highest)
                    prob = exps * (1.0 / jnp.sum(exps, axis=0, keepdims=True))
                    prob_grad = dot_nt(values[:upto], g).astype(BF16).astype(F32)
                    weighted = prob * prob_grad
                    mean = jnp.sum(weighted, axis=0, keepdims=True)
                    score_grad = (weighted - prob * mean).astype(BF16)
                    found.append((dot_nn(score_grad, q), dot_nn(prob.astype(BF16), g)))
                for kv_at, factor in ((0, HD ** (-0.5)), (1, 1.0)):
                    early, late = found[0][kv_at], found[1][kv_at]
                    grad = jnp.concatenate([(late[:half] + early) * factor, late[half:] * factor], axis=0)
                    grads[h * wide + kv_at * HD : h * wide + (kv_at + 1) * HD, token] = grad.T.astype(BF16)
            return carry

        lax.fori_loop(0, 2 * seqs, one, 0)

        leaving = []
        for k in [last] + list(range(last))[::-1]:
            total = dot_nn(grads[:, :tokens], held[k, 0]) + dot_nn(grads[:, tokens:], held[k, 1])
            total = (total * inv_root).astype(BF16)
            for h in range(heads):
                done[h, k] = total[h * wide : (h + 1) * wide]
                if k < last:
                    leaving.append(pltpu.make_async_copy(done.at[h, k], sum_refs[h].at[k], out_sems.at[h, k]))
                else:
                    for at, ref in enumerate((up_refs[h], down_refs[h])):
                        there = done.at[h, k, pl.ds(at * HD, HD)]
                        leaving.append(pltpu.make_async_copy(there, ref, out_sems.at[h, k + at]))
            for copy in leaving[-heads if k < last else -2 * heads :]:
                copy.start()
        for copy in leaving:
            copy.wait()

    any_spec = pl.BlockSpec(memory_space=pl.ANY)
    inputs = [rows_mine, rows_other, queries, queries_other, out_grad, out_grad_other]
    for h in range(heads):
        inputs += blocks[h]
    flops = 2 * 2 * tokens * chips * part * wide * heads * 2 + heads * 2 * seqs * repeat * length * length * HD * 16
    outs = call(
        body,
        [jax.ShapeDtypeStruct((last, wide, part), BF16)] * heads + [jax.ShapeDtypeStruct((HD, part), BF16)] * (2 * heads),
        [any_spec] * len(inputs),
        [any_spec] * (3 * heads),
        scratch=[
            pltpu.VMEM((chips, 2, tokens, part), BF16),
            pltpu.VMEM((heads, chips, part, wide), BF16),
            pltpu.VMEM((2 * seqs, length, own_width), BF16),
            pltpu.VMEM((2 * seqs, length, own_width), BF16),
            pltpu.VMEM((heads, 2 * tokens, wide), F32),
            pltpu.VMEM((heads * wide, 2 * tokens), BF16),
            pltpu.VMEM((heads, chips, wide, part), BF16),
            pltpu.SemaphoreType.DMA((chips, 2)),
            pltpu.SemaphoreType.DMA((heads, chips)),
            pltpu.SemaphoreType.DMA((4,)),
            pltpu.SemaphoreType.DMA((heads, chips + 1)),
        ],
        flops=flops,
        moved=2 * tokens * chips * part * 6,
        name="group_step",
    )(scalars, *inputs)
    return outs[:heads], outs[heads : 2 * heads], outs[2 * heads :]


def add_partials(scalars, own, up, down, distance, name):
    part = own.shape[-1]
    is_half = up.shape[0] == HD
    at = 2 * distance - 1

    def body(s, ou_ref, od_ref, ui_ref, di_ref, up_ref, down_ref):
        mine_up, mine_down = ou_ref[0].astype(F32), od_ref[0].astype(F32)
        if is_half:
            keys = pl.program_id(0) == 0
            up_ref[...] = jnp.where(keys, mine_up + ui_ref[...].astype(F32), mine_up).astype(BF16)
            down_ref[...] = jnp.where(keys, mine_down, mine_down + di_ref[...].astype(F32)).astype(BF16)
        else:
            up_ref[...] = (mine_up + ui_ref[...].astype(F32)).astype(BF16)
            down_ref[...] = (mine_down + di_ref[...].astype(F32)).astype(BF16)

    block = (HD, part)
    came = whole(block) if is_half else pl.BlockSpec(block, lambda i, s: (i, 0))
    shape = jax.ShapeDtypeStruct((2 * HD, part), BF16)
    return call(
        body,
        [shape] * 2,
        [
            pl.BlockSpec((1, HD, part), lambda i, s: (at, i, 0)),
            pl.BlockSpec((1, HD, part), lambda i, s: (at + 1, i, 0)),
            came,
            came,
        ],
        [pl.BlockSpec(block, lambda i, s: (i, 0))] * 2,
        grid=(2,),
        moved=2 * HD * part * 12,
        name=name,
    )(scalars, own, own, up, down)


def split_packs(values):
    deep = values.shape[0] // 2
    rows = values.shape[1] // 2
    return [
        jnp.concatenate([values[:deep, k * rows : (k + 1) * rows], values[deep:, k * rows : (k + 1) * rows]], axis=1)
        for k in range(2)
    ]


def code_deltas(scalars, own, up, down, delta_start, name):
    part = own.shape[-1]

    def body(s, g_ref, ui_ref, di_ref, d_ref, own_ref, core_ref, y_ref, far_ref):
        core = s[0]
        total = g_ref[0].astype(F32) + ui_ref[...].astype(F32) + di_ref[...].astype(F32)
        delta = d_ref[...] + inner_rate * total
        scales, coded = [], []
        for kv in range(2):
            piece = delta[kv * HD : (kv + 1) * HD]
            scale = (jnp.max(jnp.abs(piece), axis=0, keepdims=True) + scale_eps).astype(BF16).astype(F32)
            scales.append(scale)
            coded.append(piece / scale)
        grads = split_packs(total)
        codes = split_packs(jnp.concatenate(coded, axis=0))
        levels = split_packs(jnp.concatenate(scales, axis=0))
        for mine, wide_ref, thin_ref in ((True, own_ref, y_ref), (False, core_ref, far_ref)):
            first = (core == 0) if mine else (core == 1)
            grad = jnp.where(first, grads[0], grads[1]).astype(BF16)
            code = jnp.where(first, codes[0], codes[1]).astype(BF16)
            level = jnp.where(first, levels[0], levels[1])
            level = jnp.broadcast_to(level, (SCALE_ROWS, part)).astype(BF16)
            wide_ref[:HD, :] = code
            wide_ref[HD : HD + SCALE_ROWS, :] = level
            wide_ref[HD + SCALE_ROWS :, :] = grad
            thin_ref[:HD, :] = code
            thin_ref[HD:, :] = level

    wide, thin = (2 * HD + SCALE_ROWS, part), (HD + SCALE_ROWS, part)
    return call(
        body,
        [jax.ShapeDtypeStruct(shape, BF16) for shape in (wide, wide, thin, thin)],
        [
            pl.BlockSpec((1, 2 * HD, part), lambda i, s: (0, 0, 0)),
            whole(up.shape),
            whole(down.shape),
            whole(delta_start.shape),
        ],
        [whole(wide), whole(wide), whole(thin), whole(thin)],
        moved=2 * HD * part * 16,
        name=name,
    )(scalars, own, up, down, delta_start)


def finish(scalars, weight, outer, momentum, grads, codes, before, head, heads):
    rows, cols = weight.shape
    groups = len(codes[0])
    packs = [*codes[0], grads[0], *codes[1], grads[1]]
    kept = [] if before is None else list(before)
    count = len(packs)

    def body(s, w_ref, k_ref, m_ref, *refs):
        pack_refs = refs[:count]
        out_refs = refs[count + len(kept) : count + len(kept) + 3]
        refs = refs[count + len(kept) + 3 :]
        pack_held = refs[:count]
        w_held, k_held, m_held, blend, stepped, moved, pack_sems, in_sems, out_sems = refs[count:]

        def columns(at):
            core = s[0] if at < 2 else 1 - s[0]
            return pl.ds(columns_of(core, head, at % 2, heads, cols // 2), HD)

        pack_waits = [pltpu.make_async_copy(x, y, pack_sems.at[k]) for k, (x, y) in enumerate(zip(pack_refs, pack_held))]
        waits = []
        for at in range(4):
            held = ((w_ref, w_held), (k_ref, k_held), (m_ref, m_held))
            waits.append([pltpu.make_async_copy(x.at[:, columns(at)], y.at[at], in_sems.at[at, k]) for k, (x, y) in enumerate(held)])
        for copy in pack_waits[: count // 2] + waits[0] + waits[1] + pack_waits[count // 2 :] + waits[2] + waits[3]:
            copy.start()
        leaving = []
        for at in range(4):
            side, kv = at // 2, at % 2
            own = range(side * (groups + 1), (side + 1) * (groups + 1))
            if kv == 0:
                for k in own:
                    pack_waits[k].wait()
            lanes = slice(kv * rows, (kv + 1) * rows)
            grad = pack_held[own[-1]][HD + SCALE_ROWS :, lanes].astype(F32).T
            total = jnp.zeros((HD, rows), F32)
            for k in own[:-1]:
                total = total + pack_held[k][:HD, lanes].astype(F32) * pack_held[k][HD : HD + 1, lanes].astype(F32)
            average = (total / groups).T
            for copy in waits[at]:
                copy.wait()
            fresh = w_held[at].astype(F32) - inner_rate * grad
            moment = momentum_decay * m_held[at] + average
            new = k_held[at] - outer_rate * (momentum_decay * moment + average)
            moved[at] = moment
            stepped[at] = new
            blend[at] = (blend_share * fresh + (1.0 - blend_share) * new).astype(BF16)
            for k, (x, y) in enumerate(zip((blend, stepped, moved), out_refs)):
                leaving.append(pltpu.make_async_copy(x.at[at], y.at[:, columns(at)], out_sems.at[at, k]))
                leaving[-1].start()
        for copy in leaving:
            copy.wait()

    any_spec = pl.BlockSpec(memory_space=pl.ANY)
    return call(
        body,
        [
            jax.ShapeDtypeStruct((rows, cols), BF16),
            jax.ShapeDtypeStruct((rows, cols), F32),
            jax.ShapeDtypeStruct((rows, cols), F32),
        ],
        [any_spec] * (3 + count + len(kept)),
        [any_spec] * 3,
        scratch=[pltpu.VMEM(p.shape, BF16) for p in packs]
        + [pltpu.VMEM((4, rows, HD), t) for t in (BF16, F32, F32, BF16, F32, F32)]
        + [
            pltpu.SemaphoreType.DMA((count,)),
            pltpu.SemaphoreType.DMA((4, 3)),
            pltpu.SemaphoreType.DMA((4, 3)),
        ],
        moved=rows * cols * 12,
        aliases={4 + count + k: k for k in range(len(kept))},
        name=f"finish_{head}",
    )(scalars, weight, outer, momentum, *packs, *kept)


def local(hidden, norm_gain, queries, out_grad, kv_inner, kv_outer, momentum):
    count = lax.axis_size("fsdp")
    groups = lax.axis_size("group")
    index = lax.axis_index("fsdp")
    group = lax.axis_index("group")
    chips = count // 2
    far = chips // 2
    ring = ring_order(chips)
    place = {chip: at for at, chip in enumerate(ring)}
    order = [0] + [k % chips for step in range(1, far) for k in (step, -step)] + [far]
    walks = np.array([[ring[(place[j] + k) % chips] for k in order] for j in range(chips)], np.int32)
    core = index % 2
    scalars = jnp.concatenate([core[None].astype(jnp.int32), jnp.asarray(walks)[index // 2]])

    def around(shift):
        return [(2 * j + c, 2 * ring[(place[j] + shift) % chips] + c) for j in range(chips) for c in range(2)]

    up = functools.partial(lax.ppermute, axis_name="fsdp", perm=around(1))
    down = functools.partial(lax.ppermute, axis_name="fsdp", perm=around(-1))
    swap = functools.partial(lax.ppermute, axis_name="fsdp", perm=[(i, i ^ 1) for i in range(count)])

    def across(values, shift, flip):
        pairs = [
            (g * count + i, (g + shift) % groups * count + (i ^ flip)) for g in range(groups) for i in range(count)
        ]
        return lax.ppermute(values, ("group", "fsdp"), pairs)

    weight = kv_inner[0]
    rows, cols = weight.shape
    heads = cols // 2 // HD // 2
    seqs, length, width = hidden.shape[1:]
    part = 2 * rows

    received = swap(weight)
    own = own_blocks(scalars, weight, received, heads)

    tied = lax.optimization_barrier
    own, outer_other = tied((own, swap(kv_outer)))
    queries_other = swap(tied((queries[0], received))[0])
    out_grad_other = swap(tied((out_grad[0], own))[0])
    rows_mine = norm_rows(scalars, tied((hidden, own))[0].reshape(seqs * length, width), norm_gain, chips)

    blocks = [[own[h]] for h in range(heads)]
    ups, downs = list(own), list(own)
    for step in range(1, far + 1):
        for h in range(heads):
            if step < far:
                ups[h], downs[h] = up(ups[h]), down(downs[h])
                blocks[h] += [downs[h], ups[h]]
            else:
                blocks[h].append(up(ups[h]) if h % 2 == 0 else down(downs[h]))
        if step == 1:
            rows_other = swap(tied((rows_mine, queries_other, out_grad_other, ups, downs))[0])
    deltas = start_deltas(scalars, own, kv_outer, outer_other, heads)

    rows_mine, deltas = lax.optimization_barrier((rows_mine, deltas))
    sums, far_up, far_down = group_step(
        scalars, rows_mine, rows_other, blocks, queries[0], queries_other, out_grad[0], out_grad_other, heads
    )

    outs = None
    for h in range(heads):
        going_up, going_down = far_up[h], far_down[h]
        for distance in range(far - 1, 0, -1):
            going_up, going_down = add_partials(
                scalars, sums[h], up(going_up), down(going_down), distance, f"add_{h}_{distance}"
            )
        own_pack, core_pack, thin_own, thin_core = code_deltas(
            scalars, sums[h], up(going_up), down(going_down), deltas[h], f"code_{h}"
        )
        from_core = swap(core_pack)
        mine = [own_pack] + [across(thin_own, k, 0) for k in range(1, groups)]
        theirs = [from_core] + [across(thin_core, k, 1) for k in range(1, groups)]
        if groups > 2:
            deep = HD + SCALE_ROWS
            ordered = []
            for packs in (mine, theirs):
                stacked = jnp.stack([p[:deep] for p in packs])
                ordered.append([stacked[(group - g) % groups] for g in range(groups)])
            mine, theirs = ordered
        outs = finish(
            scalars, weight, kv_outer, momentum, (own_pack, from_core), (mine, theirs), outs, h, heads
        )

    blended, outer_new, momentum_new = outs
    return (blended[None], outer_new, momentum_new)


def solution(mesh):
    in_specs = (
        P("group", "fsdp", None, None),
        P(),
        P("group", "fsdp", None, None),
        P("group", "fsdp", None, None),
        P("group", "fsdp", None),
        P("fsdp", None),
        P("fsdp", None),
    )
    out_specs = (P("group", "fsdp", None), P("fsdp", None), P("fsdp", None))
    return jax.shard_map(local, mesh=mesh, in_specs=in_specs, out_specs=out_specs, check_vma=False)
```

```python
import functools

import jax
import jax.numpy as jnp
import numpy as np
from jax import lax
from jax.experimental import pallas as pl
from jax.experimental.pallas import tpu as pltpu
from jax.sharding import PartitionSpec as P

HD = 128

inner_rate = 0.25
outer_rate = 0.7
momentum_decay = 0.9
blend_share = 0.5
norm_eps = 1e-06
scale_eps = 1e-06

F32 = jnp.float32
BF16 = jnp.bfloat16
VMEM_LIMIT = 64 * 1024 * 1024 - 65536
SCALE_ROWS = 16


def ring_order(count):
    return list(range(0, count, 2)) + list(range(1, count, 2))[::-1]


def call(body, out_shape, in_specs, out_specs, grid=(1,), scratch=(), flops=0, moved=0, aliases=None, name=None):
    return pl.pallas_call(
        body,
        out_shape=out_shape,
        grid_spec=pltpu.PrefetchScalarGridSpec(
            num_scalar_prefetch=1,
            grid=grid,
            in_specs=in_specs,
            out_specs=out_specs,
            scratch_shapes=list(scratch),
        ),
        compiler_params=pltpu.CompilerParams(
            vmem_limit_bytes=VMEM_LIMIT, dimension_semantics=("arbitrary",) * len(grid)
        ),
        cost_estimate=pl.CostEstimate(flops=int(flops), bytes_accessed=int(moved), transcendentals=0),
        input_output_aliases=aliases or {},
        name=name,
    )


def whole(shape):
    zeros = (0,) * len(shape)
    return pl.BlockSpec(shape, lambda i, s: zeros)


def dot_nn(a, b):
    return lax.dot_general(a, b, (((1,), (0,)), ((), ())), preferred_element_type=F32)


def dot_nt(a, b):
    return lax.dot_general(a, b, (((1,), (1,)), ((), ())), preferred_element_type=F32)


def dot_tn(a, b):
    return lax.dot_general(a, b, (((0,), (0,)), ((), ())), preferred_element_type=F32)


def norm_rows(scalars, hidden_rows, norm_gain, chips):
    tokens, width = hidden_rows.shape
    part = width // chips
    tile = 256

    def body(s, x_ref, g_ref, o_ref):
        total = jnp.zeros((tile, 1), F32)
        for b in range(chips):
            x = x_ref[:, b * part : (b + 1) * part].astype(F32)
            total = total + jnp.sum(x * x, axis=-1, keepdims=True)
        factor = lax.rsqrt(total * (1.0 / width) + norm_eps)
        for b in range(chips):
            x = x_ref[:, b * part : (b + 1) * part].astype(F32)
            o_ref[b] = (x * factor * g_ref[:, b * part : (b + 1) * part]).astype(BF16)

    return call(
        body,
        jax.ShapeDtypeStruct((chips, tokens, part), BF16),
        [pl.BlockSpec((tile, width), lambda i, s: (i, 0)), whole((1, width))],
        pl.BlockSpec((chips, tile, part), lambda i, s: (0, i, 0)),
        grid=(tokens // tile,),
        flops=tokens * width * 6,
        moved=tokens * width * 4,
        name="norm",
    )(scalars, hidden_rows, norm_gain.reshape(1, width))


def columns_of(core, head, kv, heads, kv_width):
    return pl.multiple_of(kv * kv_width + (core * heads + head) * HD, HD)


def own_blocks(scalars, weight, received, heads):
    rows, cols = weight.shape

    def body(s, w_ref, r_ref, *o_refs):
        core = s[0]
        mine = pl.multiple_of(core * rows, 16)
        theirs = pl.multiple_of((1 - core) * rows, 16)
        for h in range(heads):
            for kv in range(2):
                there = pl.ds(columns_of(core, h, kv, heads, cols // 2), HD)
                lanes = slice(kv * HD, (kv + 1) * HD)
                o_refs[h][pl.ds(mine, rows), lanes] = w_ref[:, there]
                o_refs[h][pl.ds(theirs, rows), lanes] = r_ref[:, there]

    shape = (2 * rows, 2 * HD)
    return call(
        body,
        [jax.ShapeDtypeStruct(shape, weight.dtype)] * heads,
        [whole((rows, cols))] * 2,
        [whole(shape)] * heads,
        moved=rows * cols * 6,
        name="own_blocks",
    )(scalars, weight, received)


def start_deltas(scalars, blocks, outer, received, heads):
    rows, cols = outer.shape

    def body(s, o_ref, r_ref, *refs):
        core = s[0]
        for h in range(heads):
            block_ref, out_ref = refs[h], refs[heads + h]
            for kv in range(2):
                there = pl.ds(columns_of(core, h, kv, heads, cols // 2), HD)
                mine = o_ref[:, there]
                theirs = r_ref[:, there]
                first = jnp.where(core == 0, mine, theirs)
                second = jnp.where(core == 0, theirs, mine)
                both = jnp.concatenate([first, second], axis=0)
                both = both - block_ref[:, kv * HD : (kv + 1) * HD].astype(F32)
                out_ref[kv * HD : (kv + 1) * HD, :] = both.T

    return call(
        body,
        [jax.ShapeDtypeStruct((2 * HD, 2 * rows), F32)] * heads,
        [whole((rows, cols))] * 2 + [whole((2 * rows, 2 * HD))] * heads,
        [whole((2 * HD, 2 * rows))] * heads,
        moved=rows * cols * 14,
        name="start_deltas",
    )(scalars, outer, received, *blocks)


def group_step(scalars, rows_mine, rows_other, blocks, queries, queries_other, out_grad, out_grad_other, heads):
    chips, tokens, part = rows_mine.shape
    seqs, length, query_width = queries.shape
    own_width = query_width // 2
    repeat = own_width // (heads * HD)
    inv_root = (chips * part) ** (-0.5)
    half = length // 2
    last = chips - 1
    two_power = HD ** (-0.5) * 1.4426950408889634
    wide = 2 * HD

    def body(s, a_ref, b_ref, qa_ref, qb_ref, ga_ref, gb_ref, *refs):
        block_refs = [refs[h * chips : (h + 1) * chips] for h in range(heads)]
        refs = refs[heads * chips :]
        sum_refs, up_refs, down_refs = refs[:heads], refs[heads : 2 * heads], refs[2 * heads : 3 * heads]
        held, w_held, q_held, g_held, acc, grads, done = refs[3 * heads : 3 * heads + 7]
        row_sems, w_sems, q_sems, out_sems = refs[3 * heads + 7 :]

        waits = []
        for k in range(chips):
            wait = []
            for side, ref in enumerate((a_ref, b_ref)):
                wait.append(pltpu.make_async_copy(ref.at[s[1 + k]], held.at[k, side], row_sems.at[k, side]))
            for h in range(heads):
                wait.append(pltpu.make_async_copy(block_refs[h][k], w_held.at[h, k], w_sems.at[h, k]))
            waits.append(wait)
        mine = pl.ds(pl.multiple_of(s[0] * own_width, HD), own_width)
        pairs = (
            (qa_ref.at[:, :, mine], q_held.at[pl.ds(0, seqs)]),
            (ga_ref.at[:, :, mine], g_held.at[pl.ds(0, seqs)]),
            (qb_ref.at[:, :, mine], q_held.at[pl.ds(seqs, seqs)]),
            (gb_ref.at[:, :, mine], g_held.at[pl.ds(seqs, seqs)]),
        )
        query_waits = [pltpu.make_async_copy(x, y, q_sems.at[k]) for k, (x, y) in enumerate(pairs)]
        ahead = 3
        waits.append(query_waits)
        for k in range(ahead):
            for copy in waits[k]:
                copy.start()

        for k in range(chips):
            if k + ahead <= chips:
                for copy in waits[k + ahead]:
                    copy.start()
            for copy in waits[k]:
                copy.wait()
            for h in range(heads):
                for side in range(2):
                    here = slice(side * tokens, (side + 1) * tokens)
                    product = dot_nn(held[k, side], w_held[h, k])
                    acc[h, here, :] = product if k == 0 else acc[h, here, :] + product
        for copy in query_waits:
            copy.wait()

        def one(at, carry):
            token = pl.ds(pl.multiple_of(at * length, length), length)
            for h in range(heads):
                kv = (acc[h, token, :] * inv_root).astype(BF16)
                keys, values = kv[:, :HD], kv[:, HD:]
                found = []
                for t in range(2):
                    upto = (t + 1) * half
                    rows_of = slice(t * half, upto)
                    lanes = [slice((h * repeat + r) * HD, (h * repeat + r + 1) * HD) for r in range(repeat)]
                    q = jnp.concatenate([q_held[at, rows_of, x] for x in lanes], axis=0)
                    g = jnp.concatenate([g_held[at, rows_of, x] for x in lanes], axis=0)
                    scores = dot_nt(keys[:upto], q) * two_power
                    causal = lax.broadcasted_iota(jnp.int32, (half, half), 0) <= lax.broadcasted_iota(
                        jnp.int32, (half, half), 1
                    )
                    causal = jnp.concatenate([causal.astype(F32)] * repeat, axis=1) > 0.0
                    end = jnp.where(causal, scores[upto - half :], -1e30)
                    scores = end if t == 0 else jnp.concatenate([scores[:half], end], axis=0)
                    highest = jnp.max(scores, axis=0, keepdims=True)
                    exps = jnp.exp2(scores - highest)
                    prob = exps * (1.0 / jnp.sum(exps, axis=0, keepdims=True))
                    prob_grad = dot_nt(values[:upto], g).astype(BF16).astype(F32)
                    weighted = prob * prob_grad
                    mean = jnp.sum(weighted, axis=0, keepdims=True)
                    score_grad = (weighted - prob * mean).astype(BF16)
                    found.append((dot_nn(score_grad, q), dot_nn(prob.astype(BF16), g)))
                for kv_at, factor in ((0, HD ** (-0.5)), (1, 1.0)):
                    early, late = found[0][kv_at], found[1][kv_at]
                    grad = jnp.concatenate([(late[:half] + early) * factor, late[half:] * factor], axis=0)
                    grads[h * wide + kv_at * HD : h * wide + (kv_at + 1) * HD, token] = grad.T.astype(BF16)
            return carry

        lax.fori_loop(0, 2 * seqs, one, 0, unroll=True)

        leaving = []
        for k in [last] + list(range(last))[::-1]:
            total = dot_nn(grads[:, :tokens], held[k, 0]) + dot_nn(grads[:, tokens:], held[k, 1])
            total = (total * inv_root).astype(BF16)
            for h in range(heads):
                done[h, k] = total[h * wide : (h + 1) * wide]
                if k < last:
                    leaving.append(pltpu.make_async_copy(done.at[h, k], sum_refs[h].at[k], out_sems.at[h, k]))
                else:
                    for at, ref in enumerate((up_refs[h], down_refs[h])):
                        there = done.at[h, k, pl.ds(at * HD, HD)]
                        leaving.append(pltpu.make_async_copy(there, ref, out_sems.at[h, k + at]))
            for copy in leaving[-heads if k < last else -2 * heads :]:
                copy.start()
        for copy in leaving:
            copy.wait()

    any_spec = pl.BlockSpec(memory_space=pl.ANY)
    inputs = [rows_mine, rows_other, queries, queries_other, out_grad, out_grad_other]
    for h in range(heads):
        inputs += blocks[h]
    flops = 2 * 2 * tokens * chips * part * wide * heads * 2 + heads * 2 * seqs * repeat * length * length * HD * 16
    outs = call(
        body,
        [jax.ShapeDtypeStruct((last, wide, part), BF16)] * heads + [jax.ShapeDtypeStruct((HD, part), BF16)] * (2 * heads),
        [any_spec] * len(inputs),
        [any_spec] * (3 * heads),
        scratch=[
            pltpu.VMEM((chips, 2, tokens, part), BF16),
            pltpu.VMEM((heads, chips, part, wide), BF16),
            pltpu.VMEM((2 * seqs, length, own_width), BF16),
            pltpu.VMEM((2 * seqs, length, own_width), BF16),
            pltpu.VMEM((heads, 2 * tokens, wide), F32),
            pltpu.VMEM((heads * wide, 2 * tokens), BF16),
            pltpu.VMEM((heads, chips, wide, part), BF16),
            pltpu.SemaphoreType.DMA((chips, 2)),
            pltpu.SemaphoreType.DMA((heads, chips)),
            pltpu.SemaphoreType.DMA((4,)),
            pltpu.SemaphoreType.DMA((heads, chips + 1)),
        ],
        flops=flops,
        moved=2 * tokens * chips * part * 6,
        name="group_step",
    )(scalars, *inputs)
    return outs[:heads], outs[heads : 2 * heads], outs[2 * heads :]


def add_partials(scalars, own, up, down, distance, name):
    part = own.shape[-1]
    is_half = up.shape[0] == HD
    at = 2 * distance - 1

    def body(s, ou_ref, od_ref, ui_ref, di_ref, up_ref, down_ref):
        mine_up, mine_down = ou_ref[0].astype(F32), od_ref[0].astype(F32)
        if is_half:
            keys = pl.program_id(0) == 0
            up_ref[...] = jnp.where(keys, mine_up + ui_ref[...].astype(F32), mine_up).astype(BF16)
            down_ref[...] = jnp.where(keys, mine_down, mine_down + di_ref[...].astype(F32)).astype(BF16)
        else:
            up_ref[...] = (mine_up + ui_ref[...].astype(F32)).astype(BF16)
            down_ref[...] = (mine_down + di_ref[...].astype(F32)).astype(BF16)

    block = (HD, part)
    came = whole(block) if is_half else pl.BlockSpec(block, lambda i, s: (i, 0))
    shape = jax.ShapeDtypeStruct((2 * HD, part), BF16)
    return call(
        body,
        [shape] * 2,
        [
            pl.BlockSpec((1, HD, part), lambda i, s: (at, i, 0)),
            pl.BlockSpec((1, HD, part), lambda i, s: (at + 1, i, 0)),
            came,
            came,
        ],
        [pl.BlockSpec(block, lambda i, s: (i, 0))] * 2,
        grid=(2,),
        moved=2 * HD * part * 12,
        name=name,
    )(scalars, own, own, up, down)


def split_packs(values):
    deep = values.shape[0] // 2
    rows = values.shape[1] // 2
    return [
        jnp.concatenate([values[:deep, k * rows : (k + 1) * rows], values[deep:, k * rows : (k + 1) * rows]], axis=1)
        for k in range(2)
    ]


def code_deltas(scalars, own, up, down, delta_start, name):
    part = own.shape[-1]

    def body(s, g_ref, ui_ref, di_ref, d_ref, own_ref, core_ref, y_ref, far_ref):
        core = s[0]
        total = g_ref[0].astype(F32) + ui_ref[...].astype(F32) + di_ref[...].astype(F32)
        delta = d_ref[...] + inner_rate * total
        scales, coded = [], []
        for kv in range(2):
            piece = delta[kv * HD : (kv + 1) * HD]
            scale = (jnp.max(jnp.abs(piece), axis=0, keepdims=True) + scale_eps).astype(BF16).astype(F32)
            scales.append(scale)
            coded.append(piece / scale)
        grads = split_packs(total)
        codes = split_packs(jnp.concatenate(coded, axis=0))
        levels = split_packs(jnp.concatenate(scales, axis=0))
        for mine, wide_ref, thin_ref in ((True, own_ref, y_ref), (False, core_ref, far_ref)):
            first = (core == 0) if mine else (core == 1)
            grad = jnp.where(first, grads[0], grads[1]).astype(BF16)
            code = jnp.where(first, codes[0], codes[1]).astype(BF16)
            level = jnp.where(first, levels[0], levels[1])
            level = jnp.broadcast_to(level, (SCALE_ROWS, part)).astype(BF16)
            wide_ref[:HD, :] = code
            wide_ref[HD : HD + SCALE_ROWS, :] = level
            wide_ref[HD + SCALE_ROWS :, :] = grad
            thin_ref[:HD, :] = code
            thin_ref[HD:, :] = level

    wide, thin = (2 * HD + SCALE_ROWS, part), (HD + SCALE_ROWS, part)
    return call(
        body,
        [jax.ShapeDtypeStruct(shape, BF16) for shape in (wide, wide, thin, thin)],
        [
            pl.BlockSpec((1, 2 * HD, part), lambda i, s: (0, 0, 0)),
            whole(up.shape),
            whole(down.shape),
            whole(delta_start.shape),
        ],
        [whole(wide), whole(wide), whole(thin), whole(thin)],
        moved=2 * HD * part * 16,
        name=name,
    )(scalars, own, up, down, delta_start)


def finish(scalars, weight, outer, momentum, grads, codes, before, head, heads):
    rows, cols = weight.shape
    groups = len(codes[0])
    packs = [*codes[0], grads[0], *codes[1], grads[1]]
    kept = [] if before is None else list(before)
    count = len(packs)

    def body(s, w_ref, k_ref, m_ref, *refs):
        pack_refs = refs[:count]
        out_refs = refs[count + len(kept) : count + len(kept) + 3]
        refs = refs[count + len(kept) + 3 :]
        pack_held = refs[:count]
        w_held, k_held, m_held, blend, stepped, moved, pack_sems, in_sems, out_sems = refs[count:]

        def columns(at):
            core = s[0] if at < 2 else 1 - s[0]
            return pl.ds(columns_of(core, head, at % 2, heads, cols // 2), HD)

        pack_waits = [pltpu.make_async_copy(x, y, pack_sems.at[k]) for k, (x, y) in enumerate(zip(pack_refs, pack_held))]
        waits = []
        for at in range(4):
            held = ((w_ref, w_held), (k_ref, k_held), (m_ref, m_held))
            waits.append([pltpu.make_async_copy(x.at[:, columns(at)], y.at[at], in_sems.at[at, k]) for k, (x, y) in enumerate(held)])
        for copy in pack_waits[: count // 2] + waits[0] + waits[1] + pack_waits[count // 2 :] + waits[2] + waits[3]:
            copy.start()
        leaving = []
        for at in range(4):
            side, kv = at // 2, at % 2
            own = range(side * (groups + 1), (side + 1) * (groups + 1))
            if kv == 0:
                for k in own:
                    pack_waits[k].wait()
            lanes = slice(kv * rows, (kv + 1) * rows)
            grad = pack_held[own[-1]][HD + SCALE_ROWS :, lanes].astype(F32).T
            total = jnp.zeros((HD, rows), F32)
            for k in own[:-1]:
                total = total + pack_held[k][:HD, lanes].astype(F32) * pack_held[k][HD : HD + 1, lanes].astype(F32)
            average = (total / groups).T
            for copy in waits[at]:
                copy.wait()
            fresh = w_held[at].astype(F32) - inner_rate * grad
            moment = momentum_decay * m_held[at] + average
            new = k_held[at] - outer_rate * (momentum_decay * moment + average)
            moved[at] = moment
            stepped[at] = new
            blend[at] = (blend_share * fresh + (1.0 - blend_share) * new).astype(BF16)
            for k, (x, y) in enumerate(zip((blend, stepped, moved), out_refs)):
                leaving.append(pltpu.make_async_copy(x.at[at], y.at[:, columns(at)], out_sems.at[at, k]))
                leaving[-1].start()
        for copy in leaving:
            copy.wait()

    any_spec = pl.BlockSpec(memory_space=pl.ANY)
    return call(
        body,
        [
            jax.ShapeDtypeStruct((rows, cols), BF16),
            jax.ShapeDtypeStruct((rows, cols), F32),
            jax.ShapeDtypeStruct((rows, cols), F32),
        ],
        [any_spec] * (3 + count + len(kept)),
        [any_spec] * 3,
        scratch=[pltpu.VMEM(p.shape, BF16) for p in packs]
        + [pltpu.VMEM((4, rows, HD), t) for t in (BF16, F32, F32, BF16, F32, F32)]
        + [
            pltpu.SemaphoreType.DMA((count,)),
            pltpu.SemaphoreType.DMA((4, 3)),
            pltpu.SemaphoreType.DMA((4, 3)),
        ],
        moved=rows * cols * 12,
        aliases={4 + count + k: k for k in range(len(kept))},
        name=f"finish_{head}",
    )(scalars, weight, outer, momentum, *packs, *kept)


def local(hidden, norm_gain, queries, out_grad, kv_inner, kv_outer, momentum):
    count = lax.axis_size("fsdp")
    groups = lax.axis_size("group")
    index = lax.axis_index("fsdp")
    group = lax.axis_index("group")
    chips = count // 2
    far = chips // 2
    ring = ring_order(chips)
    place = {chip: at for at, chip in enumerate(ring)}
    order = [0] + [k % chips for step in range(1, far) for k in (step, -step)] + [far]
    walks = np.array([[ring[(place[j] + k) % chips] for k in order] for j in range(chips)], np.int32)
    core = index % 2
    scalars = jnp.concatenate([core[None].astype(jnp.int32), jnp.asarray(walks)[index // 2]])

    def around(shift):
        return [(2 * j + c, 2 * ring[(place[j] + shift) % chips] + c) for j in range(chips) for c in range(2)]

    up = functools.partial(lax.ppermute, axis_name="fsdp", perm=around(1))
    down = functools.partial(lax.ppermute, axis_name="fsdp", perm=around(-1))
    swap = functools.partial(lax.ppermute, axis_name="fsdp", perm=[(i, i ^ 1) for i in range(count)])

    def across(values, shift, flip):
        pairs = [
            (g * count + i, (g + shift) % groups * count + (i ^ flip)) for g in range(groups) for i in range(count)
        ]
        return lax.ppermute(values, ("group", "fsdp"), pairs)

    weight = kv_inner[0]
    rows, cols = weight.shape
    heads = cols // 2 // HD // 2
    seqs, length, width = hidden.shape[1:]
    part = 2 * rows

    received = swap(weight)
    own = own_blocks(scalars, weight, received, heads)

    tied = lax.optimization_barrier
    own, outer_other = tied((own, swap(kv_outer)))
    queries_other = swap(tied((queries[0], received))[0])
    out_grad_other = swap(tied((out_grad[0], own))[0])
    rows_mine = norm_rows(scalars, tied((hidden, own))[0].reshape(seqs * length, width), norm_gain, chips)

    blocks = [[own[h]] for h in range(heads)]
    ups, downs = list(own), list(own)
    for step in range(1, far + 1):
        for h in range(heads):
            if step < far:
                ups[h], downs[h] = up(ups[h]), down(downs[h])
                blocks[h] += [downs[h], ups[h]]
            else:
                blocks[h].append(up(ups[h]) if h % 2 == 0 else down(downs[h]))
        if step == 1:
            rows_other = swap(tied((rows_mine, queries_other, out_grad_other, ups, downs))[0])
    deltas = start_deltas(scalars, own, kv_outer, outer_other, heads)

    rows_mine, deltas = lax.optimization_barrier((rows_mine, deltas))
    sums, far_up, far_down = group_step(
        scalars, rows_mine, rows_other, blocks, queries[0], queries_other, out_grad[0], out_grad_other, heads
    )

    outs = None
    for h in range(heads):
        going_up, going_down = far_up[h], far_down[h]
        for distance in range(far - 1, 0, -1):
            going_up, going_down = add_partials(
                scalars, sums[h], up(going_up), down(going_down), distance, f"add_{h}_{distance}"
            )
        own_pack, core_pack, thin_own, thin_core = code_deltas(
            scalars, sums[h], up(going_up), down(going_down), deltas[h], f"code_{h}"
        )
        from_core = swap(core_pack)
        mine = [own_pack] + [across(thin_own, k, 0) for k in range(1, groups)]
        theirs = [from_core] + [across(thin_core, k, 1) for k in range(1, groups)]
        if groups > 2:
            deep = HD + SCALE_ROWS
            ordered = []
            for packs in (mine, theirs):
                stacked = jnp.stack([p[:deep] for p in packs])
                ordered.append([stacked[(group - g) % groups] for g in range(groups)])
            mine, theirs = ordered
        outs = finish(
            scalars, weight, kv_outer, momentum, (own_pack, from_core), (mine, theirs), outs, h, heads
        )

    blended, outer_new, momentum_new = outs
    return (blended[None], outer_new, momentum_new)


def solution(mesh):
    in_specs = (
        P("group", "fsdp", None, None),
        P(),
        P("group", "fsdp", None, None),
        P("group", "fsdp", None, None),
        P("group", "fsdp", None),
        P("fsdp", None),
        P("fsdp", None),
    )
    out_specs = (P("group", "fsdp", None), P("fsdp", None), P("fsdp", None))
    return jax.shard_map(local, mesh=mesh, in_specs=in_specs, out_specs=out_specs, check_vma=False)
```
